32 devices in a mesh: groups: 2 (over y), gx: 4 (over x, core), vert: 4 (over z).
Axes of the slice: x: 2, y: 2, z: 4, core: 2. Of those that a mesh axis runs over, the one named last changes fastest.
Arguments:
- distribution: float32 [64, 16, 16, 2048], P(('groups', 'gx'), None, None, 'vert'), parts along dimension 0, may hold values from 0.05 to 2
- velocity_order: int32 [2048], P('vert'), may hold values from 0 to 2047, each once
- cell_codes: int32 [64, 16, 16], P(('groups', 'gx')), parts along dimension 0, may hold values from 0 to 2, as said below
- knudsen: float32 [2], P('groups'), parts along dimension 0, may hold values from 0.05 to 1
- inflow: float32 [8], P('groups'), parts along dimension 0, may hold values from 0.5 to 1.5
Outputs:
- evolved: float32 [64, 16, 16, 2048], P(('groups', 'gx'), None, None, 'vert'), parts along dimension 0
The draws below stay inside these ranges and needn't reach their ends.
There are 2 independent parts, one for each index of `groups`. The reference program is written for one: setup_inputs(seed, part) draws one part's arguments, and reference() takes and returns one part's arrays. A program takes and returns all parts, laid end to end along the dimension named above; an argument that names none is the same for every part. Nothing has to cross between parts.
Inputs may be any that keep to these rules, and one draw needn't show every extreme that they name: `velocity_order`: names each of the 2048 velocity grid points once. `cell_codes`: 0 marks an open cell, 1 an inflow cell, 2 a wall cell.
All inputs are finite; a program needn't handle non-finite values.
Results may differ from the reference program's by a relative error of at most 0.0003.
Values sent between devices are 32-bit elements; how exact they have to be, the bound alone decides.
A program may use at most 128 MiB of HBM per device.

```python
import math
import jax
import jax.numpy as jnp
from jax import lax

NY = 16
NZ = 16
VGX = 16
VGY = 16
VGZ = 8
STEPS = 3
V = 2048
NX = 32


def draw_cell_codes(key, part):
    raw = jax.random.randint(key, (NX, NY, NZ), 0, 16)
    return jnp.where(raw == 14, 1, jnp.where(raw == 15, 2, 0)).astype(jnp.int32)


def level_of(own_key, shape, split, low, high):
    def one(position, blocks):
        steps = jax.random.uniform(jax.random.fold_in(jax.random.fold_in(own_key, 6), position), (blocks,), jnp.float32, low / len(split), high / len(split))
        return jnp.repeat(jnp.exp(steps), shape[position] // blocks).reshape((-1,) + (1,) * (len(shape) - position - 1))

    factor_of = one(*split[0])
    for cut in split[1:]:
        factor_of = factor_of * one(*cut)
    return factor_of


def setup_inputs(seed: int = 0, part: int = 0) -> dict:
    streams_of = jax.random.split(jax.random.key(seed), 6)
    own_keys = jax.random.split(jax.random.fold_in(streams_of[5], part), 6)
    return {
        "distribution": jnp.clip(jnp.exp(math.log(2.0) - 3.6888794 * jax.random.uniform(own_keys[0], (NX, NY, NZ, V), jnp.float32) ** level_of(own_keys[0], (NX, NY, NZ, V), ((0, 4), (3, 4)), -0.2, 0.2)), 0.05, 2.0),
        "velocity_order": jax.random.permutation(streams_of[1], V).astype(jnp.int32),
        "cell_codes": draw_cell_codes(jax.random.fold_in(jax.random.fold_in(streams_of[5], part), 71), part),
        "knudsen": jnp.clip(jnp.exp(jax.random.uniform(own_keys[3], (1,), jnp.float32, math.log(0.05), math.log(1.0))), 0.05, 1.0),
        "inflow": jnp.clip(jax.random.uniform(own_keys[4], (4,), jnp.float32, 0.5, 1.5), 0.5, 1.5),
    }


def grid_velocity(index, count):
    return (index.astype(jnp.float32) + 0.5 - count / 2) * (6.0 / count)


def velocity_parts(order):
    plane = VGY * VGZ
    first = grid_velocity(order // plane, VGX)
    second = grid_velocity((order // VGZ) % VGY, VGY)
    third = grid_velocity(order % VGZ, VGZ)
    return first, second, third


def minmod(lower, upper):
    return 0.5 * (jnp.sign(lower) + jnp.sign(upper)) * jnp.minimum(jnp.abs(lower), jnp.abs(upper))


def face_change(padded, courant, dim):
    count = padded.shape[dim] - 4
    left = lax.slice_in_dim(padded, 0, count + 2, axis=dim)
    centre = lax.slice_in_dim(padded, 1, count + 3, axis=dim)
    right = lax.slice_in_dim(padded, 2, count + 4, axis=dim)
    slope = minmod(centre - left, right - centre)
    low_cell = lax.slice_in_dim(centre, 0, count + 1, axis=dim)
    high_cell = lax.slice_in_dim(centre, 1, count + 2, axis=dim)
    low_slope = lax.slice_in_dim(slope, 0, count + 1, axis=dim)
    high_slope = lax.slice_in_dim(slope, 1, count + 2, axis=dim)
    ahead = jnp.maximum(courant, 0.0)
    behind = jnp.minimum(courant, 0.0)
    flux = ahead * (low_cell + 0.5 * (1.0 - courant) * low_slope) + behind * (high_cell - 0.5 * (1.0 + courant) * high_slope)
    return lax.slice_in_dim(flux, 1, count + 1, axis=dim) - lax.slice_in_dim(flux, 0, count, axis=dim)


def reference(distribution, velocity_order, cell_codes, knudsen, inflow):
    first, second, third = velocity_parts(velocity_order)
    table = jnp.stack([jnp.ones_like(first), first, second, third, 0.5 * (first * first + second * second + third * third)], axis=1)
    inflow_shape = jnp.exp(-((first - inflow[1]) ** 2 + second * second + third * third) / (2.0 * inflow[2]))
    inflow_state = inflow[0] * inflow_shape / jnp.mean(inflow_shape)
    wall_shape = jnp.exp(-(first * first + second * second + third * third) / (2.0 * inflow[3]))
    wall_norm = jnp.mean(wall_shape)
    codes = cell_codes[..., None]
    state = distribution
    for step in range(STEPS):
        padded_x = jnp.pad(state, ((2, 2), (0, 0), (0, 0), (0, 0)))
        padded_y = jnp.pad(state, ((0, 0), (2, 2), (0, 0), (0, 0)), mode="wrap")
        padded_z = jnp.pad(state, ((0, 0), (0, 0), (2, 2), (0, 0)), mode="wrap")
        moved = state - face_change(padded_x, 0.1 * first, 0)
        moved = moved - face_change(padded_y, second / 30.0, 1)
        moved = moved - face_change(padded_z, third / 30.0, 2)
        kinetic_integrals = jnp.dot(moved.reshape(-1, V), table, precision=lax.Precision.HIGHEST, preferred_element_type=jnp.float32) / V
        kinetic_integrals = kinetic_integrals.T.reshape(5, NX, NY, NZ)
        particle_concentration = kinetic_integrals[0]
        mean_flow_xaxis = kinetic_integrals[1] / particle_concentration
        mean_flow_yaxis = kinetic_integrals[2] / particle_concentration
        mean_flow_zaxis = kinetic_integrals[3] / particle_concentration
        kinetic_heat_level = (2.0 * kinetic_integrals[4] / particle_concentration - (mean_flow_xaxis ** 2 + mean_flow_yaxis ** 2 + mean_flow_zaxis ** 2)) / 3.0
        maxwellian_width = ((first - mean_flow_xaxis[..., None]) ** 2 + (second - mean_flow_yaxis[..., None]) ** 2 + (third - mean_flow_zaxis[..., None]) ** 2)
        extent_tuple = jnp.exp(-maxwellian_width / (2.0 * kinetic_heat_level[..., None]))
        norm = jnp.mean(extent_tuple, axis=-1)
        equilibrium = particle_concentration[..., None] * extent_tuple / norm[..., None]
        rate = 0.5 * particle_concentration / (particle_concentration + knudsen[0])
        relaxed = moved + rate[..., None] * (equilibrium - moved)
        wall = particle_concentration[..., None] * wall_shape / wall_norm
        state = jnp.where(codes == 1, inflow_state, jnp.where(codes == 2, wall, relaxed))
    return state
```

```python
import functools

import jax
import jax.numpy as jnp
from jax import lax
from jax.experimental import pallas as pl
from jax.experimental.pallas import tpu as pltpu
from jax.sharding import PartitionSpec as P

VGX = 16
VGY = 16
VGZ = 8
STEPS = 3
LANES = 128
LOG2E = 1.4426950408889634
MESH = pl.DeviceIdType.MESH

H1 = 3.0 / VGX
H2 = 3.0 / VGY
H3 = 3.0 / VGZ


def minmod(lower, upper):
    return jnp.maximum(jnp.minimum(lower, upper), 0.0) + jnp.minimum(
        jnp.maximum(lower, upper), 0.0
    )


def split3(value):
    high = value.astype(jnp.bfloat16).astype(jnp.float32)
    rest = value - high
    middle = rest.astype(jnp.bfloat16).astype(jnp.float32)
    return high, middle, rest - middle


def kernel(
    rows, ny, nz, width, nx_dev, nv,
    dist, order, codes, knudsen, inflow,
    out,
    state, moved, halo_low, halo_high, mom, coef, feat, wide, cour,
    in_sem, out_sem, halo_send, halo_recv, mom_send, mom_recv,
):
    cells = ny * nz
    tiles = width // LANES
    total = float(width * nv)
    half = rows // 2
    group_cells = half * cells
    mx = lax.axis_index("gx")
    mv = lax.axis_index("vert")
    has_low = mx > 0
    has_high = mx < nx_dev - 1

    load = pltpu.make_async_copy(dist, state, in_sem)
    load.start()

    barrier = pltpu.get_barrier_semaphore()

    @pl.when(has_low)
    def _():
        pl.semaphore_signal(barrier, inc=1, device_id={"gx": mx - 1}, device_id_type=MESH)

    @pl.when(has_high)
    def _():
        pl.semaphore_signal(barrier, inc=1, device_id={"gx": mx + 1}, device_id_type=MESH)

    for p in range(1, nv):
        pl.semaphore_signal(
            barrier, inc=1, device_id={"vert": lax.rem(mv + p, nv)}, device_id_type=MESH
        )
    pl.semaphore_wait(
        barrier, nv - 1 + has_low.astype(jnp.int32) + has_high.astype(jnp.int32)
    )

    def to_low(t, source):
        return pltpu.make_async_remote_copy(
            src_ref=source.at[pl.ds(0, 2)],
            dst_ref=halo_high.at[t],
            send_sem=halo_send.at[t, 0],
            recv_sem=halo_recv.at[t, 0],
            device_id={"gx": mx - 1},
            device_id_type=MESH,
        )

    def to_high(t, source):
        return pltpu.make_async_remote_copy(
            src_ref=source.at[pl.ds(rows - 2, 2)],
            dst_ref=halo_low.at[t],
            send_sem=halo_send.at[t, 1],
            recv_sem=halo_recv.at[t, 1],
            device_id={"gx": mx + 1},
            device_id_type=MESH,
        )

    @pl.when(has_low)
    def _():
        to_low(0, dist).start()

    @pl.when(has_high)
    def _():
        to_high(0, dist).start()

    slot = order[...]
    odd1 = (2 * (slot // (VGY * VGZ)) + 1 - VGX).astype(jnp.float32)
    odd2 = (2 * ((slot // VGZ) % VGY) + 1 - VGY).astype(jnp.float32)
    odd3 = (2 * (slot % VGZ) + 1 - VGZ).astype(jnp.float32)
    ratio = (H3 / H1) ** 2
    table = jnp.concatenate(
        [
            jnp.ones_like(odd1), odd1, odd2, odd3,
            odd1 * odd1, odd2 * odd2, ratio * odd3 * odd3, jnp.zeros_like(odd1),
        ],
        axis=0,
    )
    feat[...] = jnp.concatenate([table, jnp.zeros_like(table)], axis=0).astype(jnp.bfloat16)
    keep_row = (lax.broadcasted_iota(jnp.int32, (8, LANES), 0) == 7).astype(jnp.float32)
    broad = jnp.concatenate([table, keep_row], axis=1)
    wide[...] = jnp.concatenate([broad, broad, broad, jnp.zeros_like(broad)], axis=0).astype(
        jnp.bfloat16
    )
    speeds = []
    for speed in (0.1 * H1 * odd1, (H2 / 30.0) * odd2, (H3 / 30.0) * odd3):
        gain = 0.5 * (1.0 - jnp.abs(speed)) * jnp.where(speed > 0, 1.0, -1.0)
        speeds += [speed, gain]
    cour[...] = jnp.concatenate(speeds + [jnp.zeros_like(odd1)] * 2, axis=0)

    @pl.when(jnp.logical_not(has_low))
    def _():
        halo_low[...] = jnp.zeros_like(halo_low)

    @pl.when(jnp.logical_not(has_high))
    def _():
        halo_high[...] = jnp.zeros_like(halo_high)

    load.wait()

    def constants(j, dim):
        lanes = pl.ds(pl.multiple_of(j * LANES, LANES), LANES)
        speed = jnp.broadcast_to(cour[2 * dim:2 * dim + 1, lanes], (nz, LANES))
        gain = jnp.broadcast_to(cour[2 * dim + 1:2 * dim + 2, lanes], (nz, LANES))
        return lanes, speed, gain, speed > 0

    def yz_tile(index, _):
        x = index // tiles
        lanes, speed2, gain2, ahead2 = constants(index % tiles, 1)
        _, speed3, gain3, ahead3 = constants(index % tiles, 2)

        def cell(y):
            return state[x, y % ny, :, lanes]

        f_low = cell(-2)
        f_mid = cell(-1)
        f = cell(0)
        d_low = f_mid - f_low
        d = f - f_mid
        l_low = f_mid + gain2 * minmod(d_low, d)
        f_up = cell(1)
        d_up = f_up - f
        l = f + gain2 * minmod(d, d_up)
        change = l - l_low
        for y in range(ny):
            f_next = cell(y + 2)
            d_next = f_next - f_up
            l_up = f_up + gain2 * minmod(d_up, d_next)
            change_up = l_up - l
            result = f - speed2 * jnp.where(ahead2, change, change_up)
            dz = pltpu.roll(f, nz - 1, 0) - f
            lz = f + gain3 * minmod(pltpu.roll(dz, 1, 0), dz)
            face = jnp.where(ahead3, lz, pltpu.roll(lz, nz - 1, 0))
            moved[x, y, :, lanes] = result - speed3 * (face - pltpu.roll(face, 1, 0))
            f, f_up = f_up, f_next
            d_up = d_next
            l, change = l_up, change_up
        return 0

    YU = 4

    def x_tile(t, sources, outputs, index, _):
        lanes, speed, gain, ahead = constants(index % tiles, 0)
        for k in range(YU):
            y = (index // tiles) * YU + k
            f = [ref[(*lead, y, slice(None), lanes)] for ref, lead in sources]
            d = [b - a for a, b in zip(f[:-1], f[1:])]
            l = [f[i + 1] + gain * minmod(d[i], d[i + 1]) for i in range(len(d) - 1)]
            c = [b - a for a, b in zip(l[:-1], l[1:])]
            for i, x in enumerate(outputs):
                moved[x, y, :, lanes] = moved[x, y, :, lanes] - speed * jnp.where(
                    ahead, c[i], c[i + 1]
                )
        return 0

    def layer_of(group, i):
        return i + 2 if group == 1 else i + half * (i // 2)

    def moments(t, group):
        def layer(i, _):
            x = layer_of(group, i)
            flat = moved[x].reshape(cells, width)
            high = flat.astype(jnp.bfloat16)
            low = (flat - high.astype(jnp.float32)).astype(jnp.bfloat16)
            sums = lax.dot_general(
                feat[...], high, (((1,), (1,)), ((), ())), preferred_element_type=jnp.float32
            ) + lax.dot_general(
                feat[...], low, (((1,), (1,)), ((), ())), preferred_element_type=jnp.float32
            )
            mom[t, group, mv, i] = sums[0:8]
            return 0

        lax.fori_loop(0, half, layer, 0)

    def mom_copy(t, group, p):
        return pltpu.make_async_remote_copy(
            src_ref=mom.at[t, group, mv],
            dst_ref=mom.at[t, group, mv],
            send_sem=mom_send.at[t, group, p - 1],
            recv_sem=mom_recv.at[t, group, p - 1],
            device_id={"vert": lax.rem(mv + p, nv)},
            device_id_type=MESH,
        )

    def send_moments(t, group):
        for p in range(1, nv):
            mom_copy(t, group, p).start()

    def coefficients(t, group):
        for p in range(1, nv):
            mom_copy(t, group, p).wait_recv()
        sums = []
        for i in range(half):
            layer = mom[t, group, 0, i]
            for v in range(1, nv):
                layer = layer + mom[t, group, v, i]
            sums.append(layer)
        sums = jnp.concatenate(sums, axis=1)
        weight = sums[0:1]
        density = weight / total
        inverse = 1.0 / weight
        u1 = H1 * sums[1:2] * inverse
        u2 = H2 * sums[2:3] * inverse
        u3 = H3 * sums[3:4] * inverse
        square = (H1 * H1) * (sums[4:5] + sums[5:6] + sums[6:7]) * inverse
        temperature = (square - (u1 * u1 + u2 * u2 + u3 * u3)) / 3.0
        code = codes[group]
        is_inflow = code == 1
        is_wall = code == 2
        is_open = jnp.logical_not(jnp.logical_or(is_inflow, is_wall))
        rate = 0.5 * density / (density + knudsen[0])
        zero = jnp.zeros_like(u1)
        u1 = jnp.where(is_inflow, inflow[1], jnp.where(is_wall, zero, u1))
        u2 = jnp.where(is_open, u2, zero)
        u3 = jnp.where(is_open, u3, zero)
        temperature = jnp.where(
            is_inflow, inflow[2], jnp.where(is_wall, inflow[3], temperature)
        )
        front = jnp.where(is_inflow, inflow[0], jnp.where(is_wall, density, rate * density))
        keep = jnp.where(is_open, 1.0 - rate, zero)
        sharp = (0.5 * LOG2E) / temperature

        def axis_sum(count, step, u):
            grid = lax.broadcasted_iota(jnp.int32, (count, group_cells), 0).astype(jnp.float32)
            away = (2.0 * grid + (1.0 - count)) * step - u
            return jnp.sum(jnp.exp2(-(away * away) * sharp), axis=0, keepdims=True)

        norm = axis_sum(VGX, H1, u1) * axis_sum(VGY, H2, u2) * axis_sum(VGZ, H3, u3)
        constant = jnp.log2(front * total / norm) - (u1 * u1 + u2 * u2 + u3 * u3) * sharp
        slope = 2.0 * sharp
        quad = -(H1 * H1) * sharp
        packed = jnp.concatenate(
            [
                constant, slope * u1 * H1, slope * u2 * H2, slope * u3 * H3,
                quad, quad, quad, keep,
            ],
            axis=0,
        )
        stacked = jnp.concatenate([*split3(packed), jnp.zeros_like(packed)], axis=0)
        for k in range(group_cells // LANES):
            coef[group, k] = stacked[:, k * LANES:(k + 1) * LANES].T.astype(jnp.bfloat16)

    blocks = cells // LANES
    yb = ny // blocks

    def relax(group, first, count):
        def block(k, _):
            x = layer_of(group, k // blocks)
            ys = pl.ds((k % blocks) * yb, yb)
            power = jnp.dot(coef[group, k], wide[...], preferred_element_type=jnp.float32)
            keep = power[:, width:]
            for j in range(tiles):
                lanes = slice(j * LANES, (j + 1) * LANES)
                old = moved[x, ys, :, lanes].reshape(LANES, LANES)
                new = keep * old + jnp.exp2(power[:, lanes])
                state[x, ys, :, lanes] = new.reshape(yb, nz, LANES)
            return 0

        lax.fori_loop(first * blocks, (first + count) * blocks, block, 0)

    def write_out(first):
        return pltpu.make_async_copy(
            state.at[pl.ds(first, 2)], out.at[pl.ds(first, 2)], out_sem.at[first // 2]
        )

    def step(t, _):
        last = t == STEPS - 1
        lax.fori_loop(0, rows * tiles, yz_tile, 0)
        count = (ny // YU) * tiles
        inner = [(state, (x,)) for x in range(rows)]
        lax.fori_loop(
            0, count, functools.partial(x_tile, t, inner, range(2, rows - 2)), 0
        )
        moments(t, 1)
        send_moments(t, 1)

        @pl.when(has_high)
        def _():
            to_low(t, state).wait_recv()

        @pl.when(has_low)
        def _():
            to_high(t, state).wait_recv()

        low = [(halo_low, (t, 0)), (halo_low, (t, 1))] + inner[:4]
        lax.fori_loop(0, count, functools.partial(x_tile, t, low, (0, 1)), 0)
        high = inner[-4:] + [(halo_high, (t, 0)), (halo_high, (t, 1))]
        lax.fori_loop(
            0, count, functools.partial(x_tile, t, high, (rows - 2, rows - 1)), 0
        )
        moments(t, 0)
        send_moments(t, 0)

        coefficients(t, 1)
        relax(1, 0, half)

        @pl.when(last)
        def _():
            for first in range(2, rows - 2, 2):
                write_out(first).start()

        @pl.when(has_low)
        def _():
            to_low(t, state).wait_send()

        @pl.when(has_high)
        def _():
            to_high(t, state).wait_send()

        coefficients(t, 0)
        relax(0, 0, 2)

        @pl.when(jnp.logical_and(has_low, jnp.logical_not(last)))
        def _():
            to_low(t + 1, state).start()

        relax(0, 2, 2)

        @pl.when(jnp.logical_and(has_high, jnp.logical_not(last)))
        def _():
            to_high(t + 1, state).start()

        for group in range(2):
            for p in range(1, nv):
                mom_copy(t, group, p).wait_send()
        return 0

    lax.fori_loop(0, STEPS, step, 0)
    write_out(0).start()
    write_out(rows - 2).start()
    for first in range(0, rows, 2):
        write_out(first).wait()


def body(distribution, velocity_order, cell_codes, knudsen, inflow):
    rows, ny, nz, width = distribution.shape
    nv = lax.axis_size("vert")
    nx_dev = lax.axis_size("gx")
    cells = ny * nz
    half = rows // 2
    flat = cell_codes.reshape(rows, cells)
    codes = jnp.stack(
        [
            jnp.concatenate([flat[:2], flat[-2:]]).reshape(1, -1),
            flat[2:-2].reshape(1, -1),
        ]
    )
    vmem = pl.BlockSpec(memory_space=pltpu.VMEM)
    smem = pl.BlockSpec(memory_space=pltpu.SMEM)
    hbm = pl.BlockSpec(memory_space=pl.ANY)
    return pl.pallas_call(
        functools.partial(kernel, rows, ny, nz, width, nx_dev, nv),
        out_shape=jax.ShapeDtypeStruct(distribution.shape, jnp.float32),
        in_specs=[hbm, vmem, vmem, smem, smem],
        out_specs=hbm,
        scratch_shapes=[
            pltpu.VMEM((rows, ny, nz, width), jnp.float32),
            pltpu.VMEM((rows, ny, nz, width), jnp.float32),
            pltpu.VMEM((STEPS, 2, ny, nz, width), jnp.float32),
            pltpu.VMEM((STEPS, 2, ny, nz, width), jnp.float32),
            pltpu.VMEM((STEPS, 2, nv, half, 8, cells), jnp.float32),
            pltpu.VMEM((2, half * cells // LANES, LANES, 32), jnp.bfloat16),
            pltpu.VMEM((16, width), jnp.bfloat16),
            pltpu.VMEM((32, width + LANES), jnp.bfloat16),
            pltpu.VMEM((8, width), jnp.float32),
            pltpu.SemaphoreType.DMA,
            pltpu.SemaphoreType.DMA((rows // 2,)),
            pltpu.SemaphoreType.DMA((STEPS, 2)),
            pltpu.SemaphoreType.DMA((STEPS, 2)),
            pltpu.SemaphoreType.DMA((STEPS, 2, nv - 1)),
            pltpu.SemaphoreType.DMA((STEPS, 2, nv - 1)),
        ],
        compiler_params=pltpu.CompilerParams(
            collective_id=0, has_side_effects=True, vmem_limit_bytes=48 * 1024 * 1024
        ),
    )(distribution, velocity_order.reshape(1, width), codes, knudsen, inflow)


def solution(mesh):
    placed = (
        P(("groups", "gx"), None, None, "vert"),
        P("vert"),
        P(("groups", "gx"), None, None),
        P("groups"),
        P("groups"),
    )
    return jax.shard_map(
        body,
        mesh=mesh,
        in_specs=placed,
        out_specs=P(("groups", "gx"), None, None, "vert"),
        check_vma=False,
    )
```

```python
import functools

import jax
import jax.numpy as jnp
from jax import lax
from jax.experimental import pallas as pl
from jax.experimental.pallas import tpu as pltpu
from jax.sharding import PartitionSpec as P

VGX = 16
VGY = 16
VGZ = 8
STEPS = 3
LANES = 128
LOG2E = 1.4426950408889634
MESH = pl.DeviceIdType.MESH

H1 = 3.0 / VGX
H2 = 3.0 / VGY
H3 = 3.0 / VGZ


def minmod(lower, upper):
    return jnp.maximum(jnp.minimum(lower, upper), 0.0) + jnp.minimum(
        jnp.maximum(lower, upper), 0.0
    )


def split3(value):
    high = value.astype(jnp.bfloat16).astype(jnp.float32)
    rest = value - high
    middle = rest.astype(jnp.bfloat16).astype(jnp.float32)
    return high, middle, rest - middle


def kernel(
    rows, ny, nz, width, nx_dev, nv,
    dist, order_in, codes_in, knudsen_in, inflow_in,
    out,
    state, moved, halo_low, halo_high, mom_outer, mom_inner, coef, feat, wide, cour,
    order, codes, knudsen, inflow, spread, cell_code,
    in_sem, small_sem, out_sem, halo_send, halo_recv,
    outer_send, outer_recv, inner_send, inner_recv,
):
    tiles = width // LANES
    total = float(width * nv)
    chunks = 2 * ny * nz // LANES
    yc = ny // chunks
    inner_rows = rows - 4
    inner_blocks = inner_rows * ny * nz // LANES
    yb = LANES // nz
    per_layer = ny // yb
    mx = lax.axis_index("gx")
    mv = lax.axis_index("vert")
    has_low = mx > 0
    has_high = mx < nx_dev - 1

    small = [
        pltpu.make_async_copy(source, target, small_sem.at[i])
        for i, (source, target) in enumerate(
            ((order_in, order), (codes_in, codes), (knudsen_in, knudsen), (inflow_in, inflow))
        )
    ]
    for copy in small:
        copy.start()
    load = [
        pltpu.make_async_copy(
            dist.at[pl.ds(first, count)], state.at[0, pl.ds(first, count)], in_sem.at[i]
        )
        for i, (first, count) in enumerate(((0, 2), (rows - 2, 2), (2, inner_rows)))
    ]
    for copy in load:
        copy.start()

    barrier = pltpu.get_barrier_semaphore()

    @pl.when(has_low)
    def _():
        pl.semaphore_signal(barrier, inc=1, device_id={"gx": mx - 1}, device_id_type=MESH)

    @pl.when(has_high)
    def _():
        pl.semaphore_signal(barrier, inc=1, device_id={"gx": mx + 1}, device_id_type=MESH)

    for p in range(1, nv):
        pl.semaphore_signal(
            barrier, inc=1, device_id={"vert": lax.rem(mv + p, nv)}, device_id_type=MESH
        )
    pl.semaphore_wait(
        barrier, nv - 1 + has_low.astype(jnp.int32) + has_high.astype(jnp.int32)
    )

    def to_low(t, c, source):
        ys = pl.ds(c * yc, yc)
        return pltpu.make_async_remote_copy(
            src_ref=source.at[pl.ds(0, 2), ys],
            dst_ref=halo_high.at[t, :, ys],
            send_sem=halo_send.at[t, 0, c],
            recv_sem=halo_recv.at[t, 0, c],
            device_id={"gx": mx - 1},
            device_id_type=MESH,
        )

    def to_high(t, c, source):
        ys = pl.ds(c * yc, yc)
        return pltpu.make_async_remote_copy(
            src_ref=source.at[pl.ds(rows - 2, 2), ys],
            dst_ref=halo_low.at[t, :, ys],
            send_sem=halo_send.at[t, 1, c],
            recv_sem=halo_recv.at[t, 1, c],
            device_id={"gx": mx + 1},
            device_id_type=MESH,
        )

    @pl.when(has_low)
    def _():
        for c in range(chunks):
            to_low(0, c, dist).start()

    @pl.when(has_high)
    def _():
        for c in range(chunks):
            to_high(0, c, dist).start()

    for copy in small:
        copy.wait()

    slot = order[...]
    odd1 = (2 * (slot // (VGY * VGZ)) + 1 - VGX).astype(jnp.float32)
    odd2 = (2 * ((slot // VGZ) % VGY) + 1 - VGY).astype(jnp.float32)
    odd3 = (2 * (slot % VGZ) + 1 - VGZ).astype(jnp.float32)
    ratio = (H3 / H1) ** 2
    table = jnp.concatenate(
        [
            jnp.ones_like(odd1), odd1, odd2, odd3,
            odd1 * odd1, odd2 * odd2, ratio * odd3 * odd3, jnp.zeros_like(odd1),
        ],
        axis=0,
    )
    feat[...] = jnp.concatenate([table, jnp.zeros_like(table)], axis=0).astype(jnp.bfloat16)
    keep_row = (lax.broadcasted_iota(jnp.int32, (8, LANES), 0) == 7).astype(jnp.float32)
    broad = jnp.concatenate([table, keep_row], axis=1)
    wide[...] = jnp.concatenate([broad, broad, broad, jnp.zeros_like(broad)], axis=0).astype(
        jnp.bfloat16
    )
    speeds = []
    for speed in (0.1 * H1 * odd1, (H2 / 30.0) * odd2, (H3 / 30.0) * odd3):
        gain = 0.5 * (1.0 - jnp.abs(speed)) * jnp.where(speed > 0, 1.0, -1.0)
        speeds += [speed, gain]
    cour[...] = jnp.concatenate(speeds + [jnp.zeros_like(odd1)] * 2, axis=0)

    pick = lax.broadcasted_iota(jnp.int32, (nz, LANES), 1) % nz
    pick = (pick == lax.broadcasted_iota(jnp.int32, (nz, LANES), 0)).astype(jnp.bfloat16)
    spread[...] = jnp.dot(
        codes[...].reshape(rows * ny, nz).astype(jnp.float32).astype(jnp.bfloat16),
        pick,
        preferred_element_type=jnp.float32,
    )

    def code_part(row, count, at):
        line = lax.broadcasted_iota(jnp.int32, (count, LANES), 0) + at
        lane = lax.broadcasted_iota(jnp.int32, (count, LANES), 1) // nz
        return jnp.sum(
            jnp.where(line == lane, spread[row:row + count], 0.0), axis=0, keepdims=True
        )

    for c in range(chunks):
        for side in range(2):
            row = side * (rows - 2) * ny + c * yc
            cell_code[2 * c + side] = code_part(row, yc, 0) + code_part(row + ny, yc, yc)
    for k in range(inner_blocks):
        cell_code[2 * chunks + k] = code_part(2 * ny + k * yb, yb, 0)

    @pl.when(jnp.logical_not(has_low))
    def _():
        halo_low[...] = jnp.zeros_like(halo_low)

    @pl.when(jnp.logical_not(has_high))
    def _():
        halo_high[...] = jnp.zeros_like(halo_high)

    for copy in load:
        copy.wait()

    def constants(j, dim):
        lanes = pl.ds(pl.multiple_of(j * LANES, LANES), LANES)
        speed = jnp.broadcast_to(cour[2 * dim:2 * dim + 1, lanes], (nz, LANES))
        gain = jnp.broadcast_to(cour[2 * dim + 1:2 * dim + 2, lanes], (nz, LANES))
        return lanes, speed, gain, speed > 0

    def yz_tile(now, layer, index, _):
        x = layer(index // tiles)
        lanes, speed2, gain2, ahead2 = constants(index % tiles, 1)
        _, speed3, gain3, ahead3 = constants(index % tiles, 2)

        def cell(y):
            return state[now, x, y % ny, :, lanes]

        f_low = cell(-2)
        f_mid = cell(-1)
        f = cell(0)
        d_low = f_mid - f_low
        d = f - f_mid
        l_low = f_mid + gain2 * minmod(d_low, d)
        f_up = cell(1)
        d_up = f_up - f
        l = f + gain2 * minmod(d, d_up)
        change = l - l_low
        for y in range(ny):
            f_next = cell(y + 2)
            d_next = f_next - f_up
            l_up = f_up + gain2 * minmod(d_up, d_next)
            change_up = l_up - l
            result = f - speed2 * jnp.where(ahead2, change, change_up)
            dz = pltpu.roll(f, nz - 1, 0) - f
            lz = f + gain3 * minmod(pltpu.roll(dz, 1, 0), dz)
            face = jnp.where(ahead3, lz, pltpu.roll(lz, nz - 1, 0))
            moved[x, y, :, lanes] = result - speed3 * (face - pltpu.roll(face, 1, 0))
            f, f_up = f_up, f_next
            d_up = d_next
            l, change = l_up, change_up
        return 0

    def yz(now, layer, count):
        lax.fori_loop(0, count * tiles, functools.partial(yz_tile, now, layer), 0)

    def x_tile(jobs, j, ys):
        lanes, speed, gain, ahead = constants(j, 0)
        for y in ys:
            for sources, outputs in jobs:
                f = [ref[(*lead, y, slice(None), lanes)] for ref, lead in sources]
                d = [b - a for a, b in zip(f[:-1], f[1:])]
                l = [f[i + 1] + gain * minmod(d[i], d[i + 1]) for i in range(len(d) - 1)]
                c = [b - a for a, b in zip(l[:-1], l[1:])]
                for i, x in enumerate(outputs):
                    moved[x, y, :, lanes] = moved[x, y, :, lanes] - speed * jnp.where(
                        ahead, c[i], c[i + 1]
                    )

    def x_inner(now):
        job = ([(state, (now, x)) for x in range(rows)], range(2, rows - 2))

        def tile(index, _):
            x_tile([job], index % tiles, [(index // tiles) * yc + k for k in range(yc)])
            return 0

        lax.fori_loop(0, (ny // yc) * tiles, tile, 0)

    def x_outer(t, now, chunk):
        low = [(halo_low, (t, 0)), (halo_low, (t, 1))] + [(state, (now, x)) for x in range(4)]
        high = [(state, (now, x)) for x in range(rows - 4, rows)] + [
            (halo_high, (t, 0)), (halo_high, (t, 1))
        ]
        jobs = [(low, (0, 1)), (high, (rows - 2, rows - 1))]

        def tile(j, _):
            x_tile(jobs, j, [chunk * yc + k for k in range(yc)])
            return 0

        lax.fori_loop(0, tiles, tile, 0)

    def block_moments(flat):
        high = flat.astype(jnp.bfloat16)
        low = (flat - high.astype(jnp.float32)).astype(jnp.bfloat16)
        contract = (((1,), (1,)), ((), ()))
        sums = lax.dot_general(
            feat[...], high, contract, preferred_element_type=jnp.float32
        ) + lax.dot_general(feat[...], low, contract, preferred_element_type=jnp.float32)
        return sums[0:8]

    def outer_copy(t, c, p):
        return pltpu.make_async_remote_copy(
            src_ref=mom_outer.at[t, mv, c],
            dst_ref=mom_outer.at[t, mv, c],
            send_sem=outer_send.at[t, c, p - 1],
            recv_sem=outer_recv.at[t, c, p - 1],
            device_id={"vert": lax.rem(mv + p, nv)},
            device_id_type=MESH,
        )

    def inner_copy(t, p):
        return pltpu.make_async_remote_copy(
            src_ref=mom_inner.at[t, mv],
            dst_ref=mom_inner.at[t, mv],
            send_sem=inner_send.at[t, p - 1],
            recv_sem=inner_recv.at[t, p - 1],
            device_id={"vert": lax.rem(mv + p, nv)},
            device_id_type=MESH,
        )

    def moments_outer(t, c):
        for side in range(2):
            part = moved[pl.ds(side * (rows - 2), 2), pl.ds(c * yc, yc)]
            mom_outer[t, mv, c, side] = block_moments(part.reshape(LANES, width))
        for p in range(1, nv):
            outer_copy(t, c, p).start()

    def moments_inner(t):
        def layer(i, _):
            sums = block_moments(moved[i + 2].reshape(ny * nz, width))
            for k in range(per_layer):
                mom_inner[t, mv, i * per_layer + k] = sums[:, k * LANES:(k + 1) * LANES]
            return 0

        lax.fori_loop(0, inner_rows, layer, 0)
        for p in range(1, nv):
            inner_copy(t, p).start()

    def coefficients(blocks, first):
        sums = jnp.concatenate(
            [functools.reduce(lambda a, b: a + b, parts) for parts in blocks], axis=1
        )
        count = len(blocks)
        code = jnp.concatenate([cell_code[first + k] for k in range(count)], axis=1)
        weight = sums[0:1]
        density = weight / total
        inverse = 1.0 / weight
        u1 = H1 * sums[1:2] * inverse
        u2 = H2 * sums[2:3] * inverse
        u3 = H3 * sums[3:4] * inverse
        square = (H1 * H1) * (sums[4:5] + sums[5:6] + sums[6:7]) * inverse
        temperature = (square - (u1 * u1 + u2 * u2 + u3 * u3)) / 3.0
        is_inflow = code == 1.0
        is_wall = code == 2.0
        is_open = code == 0.0
        rate = 0.5 * density / (density + knudsen[0:1, 0:1])
        zero = jnp.zeros_like(u1)
        u1 = jnp.where(is_inflow, inflow[0:1, 1:2], jnp.where(is_wall, zero, u1))
        u2 = jnp.where(is_open, u2, zero)
        u3 = jnp.where(is_open, u3, zero)
        temperature = jnp.where(
            is_inflow, inflow[0:1, 2:3], jnp.where(is_wall, inflow[0:1, 3:4], temperature)
        )
        front = jnp.where(
            is_inflow, inflow[0:1, 0:1], jnp.where(is_wall, density, rate * density)
        )
        keep = jnp.where(is_open, 1.0 - rate, zero)
        sharp = (0.5 * LOG2E) / temperature

        def axis_sum(points, spacing, u):
            grid = lax.broadcasted_iota(jnp.int32, (points, count * LANES), 0)
            away = (2.0 * grid.astype(jnp.float32) + (1.0 - points)) * spacing - u
            return jnp.sum(jnp.exp2(-(away * away) * sharp), axis=0, keepdims=True)

        norm = axis_sum(VGX, H1, u1) * axis_sum(VGY, H2, u2) * axis_sum(VGZ, H3, u3)
        constant = jnp.log2(front * total / norm) - (u1 * u1 + u2 * u2 + u3 * u3) * sharp
        slope = 2.0 * sharp
        quad = -(H1 * H1) * sharp
        packed = jnp.concatenate(
            [
                constant, slope * u1 * H1, slope * u2 * H2, slope * u3 * H3,
                quad, quad, quad, keep,
            ],
            axis=0,
        )
        stacked = jnp.concatenate([*split3(packed), jnp.zeros_like(packed)], axis=0)
        for k in range(count):
            coef[first + k] = stacked[:, k * LANES:(k + 1) * LANES].T.astype(jnp.bfloat16)

    def relax_block(then, k, xs, ys):
        power = jnp.dot(coef[k], wide[...], preferred_element_type=jnp.float32)
        keep = power[:, width:]
        for j in range(tiles):
            lanes = slice(j * LANES, (j + 1) * LANES)
            old = moved[xs, ys, :, lanes]
            new = keep * old.reshape(LANES, LANES) + jnp.exp2(power[:, lanes])
            state[then, xs, ys, :, lanes] = new.reshape(old.shape)

    def relax_outer(t, then, c):
        for p in range(1, nv):
            outer_copy(t, c, p).wait_recv()
        coefficients(
            [[mom_outer[t, v, c, side] for v in range(nv)] for side in range(2)], 2 * c
        )
        for side in range(2):
            relax_block(
                then, 2 * c + side, pl.ds(side * (rows - 2), 2), pl.ds(c * yc, yc)
            )

    def relax_inner(t, then):
        for p in range(1, nv):
            inner_copy(t, p).wait_recv()
        coefficients(
            [[mom_inner[t, v, k] for v in range(nv)] for k in range(inner_blocks)], 2 * chunks
        )

        def block(k, _):
            relax_block(
                then, 2 * chunks + k,
                pl.ds(2 + k // per_layer, 1), pl.ds((k % per_layer) * yb, yb),
            )
            return 0

        lax.fori_loop(0, inner_blocks, block, 0)

    final = STEPS % 2

    def write_inner():
        xs = pl.ds(2, inner_rows)
        return pltpu.make_async_copy(state.at[final, xs], out.at[xs], out_sem.at[0])

    def write_outer(c, side):
        xs, ys = pl.ds(side * (rows - 2), 2), pl.ds(c * yc, yc)
        return pltpu.make_async_copy(
            state.at[final, xs, ys], out.at[xs, ys], out_sem.at[1 + 2 * c + side]
        )

    def outer_layer(i):
        return i + inner_rows * (i // 2)

    def step(t, _):
        last = t == STEPS - 1
        now = t % 2
        then = 1 - now
        current = state.at[now]
        following = state.at[then]
        split = inner_rows // 2

        def fill_1():
            yz(now, lambda i: i + 2, split)

        def fill_2():
            yz(now, lambda i: i + 2 + split, inner_rows - split)

        def fill_3():
            x_inner(now)
            moments_inner(t)

        def fill_4():
            relax_inner(t, then)

        fillers = [fill_1, fill_2, fill_3, fill_4]
        yz(now, outer_layer, 4)
        for c in range(chunks):

            @pl.when(has_high)
            def _():
                to_low(t, c, current).wait_recv()

            @pl.when(has_low)
            def _():
                to_high(t, c, current).wait_recv()

            x_outer(t, now, c)
            moments_outer(t, c)
            if c < chunks - 1:
                fillers[c]()
            else:
                for fill in fillers[c:]:
                    fill()

            @pl.when(last)
            def _():
                if c == chunks - 1:
                    write_inner().start()

            relax_outer(t, then, c)

            @pl.when(jnp.logical_and(has_low, jnp.logical_not(last)))
            def _():
                to_low(t + 1, c, following).start()

            @pl.when(jnp.logical_and(has_high, jnp.logical_not(last)))
            def _():
                to_high(t + 1, c, following).start()

            @pl.when(last)
            def _():
                for side in range(2):
                    write_outer(c, side).start()

        for c in range(chunks):

            @pl.when(has_low)
            def _():
                to_low(t, c, current).wait_send()

            @pl.when(has_high)
            def _():
                to_high(t, c, current).wait_send()

            for p in range(1, nv):
                outer_copy(t, c, p).wait_send()
        for p in range(1, nv):
            inner_copy(t, p).wait_send()
        return 0

    lax.fori_loop(0, STEPS, step, 0)
    write_inner().wait()
    for c in range(chunks):
        for side in range(2):
            write_outer(c, side).wait()


def body(distribution, velocity_order, cell_codes, knudsen, inflow):
    rows, ny, nz, width = distribution.shape
    nv = lax.axis_size("vert")
    nx_dev = lax.axis_size("gx")
    chunks = 2 * ny * nz // LANES
    inner_blocks = (rows - 4) * ny * nz // LANES
    blocks = 2 * chunks + inner_blocks
    hbm = pl.BlockSpec(memory_space=pl.ANY)
    dma = pltpu.SemaphoreType.DMA
    return pl.pallas_call(
        functools.partial(kernel, rows, ny, nz, width, nx_dev, nv),
        out_shape=jax.ShapeDtypeStruct(distribution.shape, jnp.float32),
        in_specs=[pl.BlockSpec(memory_space=pltpu.HBM)] * 5,
        out_specs=hbm,
        scratch_shapes=[
            pltpu.VMEM((2, rows, ny, nz, width), jnp.float32),
            pltpu.VMEM((rows, ny, nz, width), jnp.float32),
            pltpu.VMEM((STEPS, 2, ny, nz, width), jnp.float32),
            pltpu.VMEM((STEPS, 2, ny, nz, width), jnp.float32),
            pltpu.VMEM((STEPS, nv, chunks, 2, 8, LANES), jnp.float32),
            pltpu.VMEM((STEPS, nv, inner_blocks, 8, LANES), jnp.float32),
            pltpu.VMEM((blocks, LANES, 32), jnp.bfloat16),
            pltpu.VMEM((16, width), jnp.bfloat16),
            pltpu.VMEM((32, width + LANES), jnp.bfloat16),
            pltpu.VMEM((8, width), jnp.float32),
            pltpu.VMEM((1, width), jnp.int32),
            pltpu.VMEM((rows, ny, nz), jnp.int32),
            pltpu.VMEM((1, 1), jnp.float32),
            pltpu.VMEM((1, 4), jnp.float32),
            pltpu.VMEM((rows * ny, LANES), jnp.float32),
            pltpu.VMEM((blocks, 1, LANES), jnp.float32),
            dma((3,)),
            dma((4,)),
            dma((1 + 2 * chunks,)),
            dma((STEPS, 2, chunks)),
            dma((STEPS, 2, chunks)),
            dma((STEPS, chunks, nv - 1)),
            dma((STEPS, chunks, nv - 1)),
            dma((STEPS, nv - 1)),
            dma((STEPS, nv - 1)),
        ],
        compiler_params=pltpu.CompilerParams(
            collective_id=0, has_side_effects=True, vmem_limit_bytes=48 * 1024 * 1024
        ),
    )(
        distribution,
        velocity_order.reshape(1, width),
        cell_codes,
        knudsen.reshape(1, 1),
        inflow.reshape(1, 4),
    )


def solution(mesh):
    placed = (
        P(("groups", "gx"), None, None, "vert"),
        P("vert"),
        P(("groups", "gx"), None, None),
        P("groups"),
        P("groups"),
    )
    return jax.shard_map(
        body,
        mesh=mesh,
        in_specs=placed,
        out_specs=P(("groups", "gx"), None, None, "vert"),
        check_vma=False,
    )
```

```python
import functools

import jax
import jax.numpy as jnp
from jax import lax
from jax.experimental import pallas as pl
from jax.experimental.pallas import tpu as pltpu
from jax.sharding import PartitionSpec as P

VGX = 16
VGY = 16
VGZ = 8
STEPS = 3
LANES = 128
LOG2E = 1.4426950408889634
MESH = pl.DeviceIdType.MESH

H1 = 3.0 / VGX
H2 = 3.0 / VGY
H3 = 3.0 / VGZ


def minmod(lower, upper):
    return jnp.maximum(jnp.minimum(lower, upper), jnp.minimum(jnp.maximum(lower, upper), 0.0))


def split3(value):
    high = value.astype(jnp.bfloat16).astype(jnp.float32)
    rest = value - high
    middle = rest.astype(jnp.bfloat16).astype(jnp.float32)
    return high, middle, rest - middle


def kernel(
    rows, ny, nz, width, nx_dev, nv,
    dist, order_in, codes_in, knudsen_in, inflow_in,
    out,
    state, part, moved, halo_low, halo_high, mom_outer, mom_inner, coef, feat, wide, cour,
    order, codes, knudsen, inflow, spread, cell_code,
    in_sem, small_sem, out_sem, halo_send, halo_recv,
    outer_send, outer_recv, inner_send, inner_recv,
):
    tiles = width // LANES
    total = float(width * nv)
    yc = LANES // nz
    chunks = ny // yc
    inner_rows = rows - 4
    inner_blocks = inner_rows * chunks
    outer_layers = (0, 1, rows - 2, rows - 1)
    mx = lax.axis_index("gx")
    mv = lax.axis_index("vert")
    has_low = mx > 0
    has_high = mx < nx_dev - 1

    small = [
        pltpu.make_async_copy(source, target, small_sem.at[i])
        for i, (source, target) in enumerate(
            ((order_in, order), (codes_in, codes), (knudsen_in, knudsen), (inflow_in, inflow))
        )
    ]
    for copy in small:
        copy.start()
    load = [
        pltpu.make_async_copy(
            dist.at[pl.ds(first, count)], state.at[0, pl.ds(first, count)], in_sem.at[i]
        )
        for i, (first, count) in enumerate(((0, 2), (rows - 2, 2), (2, inner_rows)))
    ]
    for copy in load:
        copy.start()

    barrier = pltpu.get_barrier_semaphore()

    @pl.when(has_low)
    def _():
        pl.semaphore_signal(barrier, inc=1, device_id={"gx": mx - 1}, device_id_type=MESH)

    @pl.when(has_high)
    def _():
        pl.semaphore_signal(barrier, inc=1, device_id={"gx": mx + 1}, device_id_type=MESH)

    for p in range(1, nv):
        pl.semaphore_signal(
            barrier, inc=1, device_id={"vert": lax.rem(mv + p, nv)}, device_id_type=MESH
        )
    pl.semaphore_wait(
        barrier, nv - 1 + has_low.astype(jnp.int32) + has_high.astype(jnp.int32)
    )

    def to_low(t, c, source):
        ys = pl.ds(c * yc, yc)
        return pltpu.make_async_remote_copy(
            src_ref=source.at[pl.ds(0, 2), ys],
            dst_ref=halo_high.at[t, :, ys],
            send_sem=halo_send.at[t, 0, c],
            recv_sem=halo_recv.at[t, 0, c],
            device_id={"gx": mx - 1},
            device_id_type=MESH,
        )

    def to_high(t, c, source):
        ys = pl.ds(c * yc, yc)
        return pltpu.make_async_remote_copy(
            src_ref=source.at[pl.ds(rows - 2, 2), ys],
            dst_ref=halo_low.at[t, :, ys],
            send_sem=halo_send.at[t, 1, c],
            recv_sem=halo_recv.at[t, 1, c],
            device_id={"gx": mx + 1},
            device_id_type=MESH,
        )

    @pl.when(has_low)
    def _():
        for c in range(chunks):
            to_low(0, c, dist).start()

    @pl.when(has_high)
    def _():
        for c in range(chunks):
            to_high(0, c, dist).start()

    for copy in small:
        copy.wait()

    slot = order[...]
    odd1 = (2 * (slot // (VGY * VGZ)) + 1 - VGX).astype(jnp.float32)
    odd2 = (2 * ((slot // VGZ) % VGY) + 1 - VGY).astype(jnp.float32)
    odd3 = (2 * (slot % VGZ) + 1 - VGZ).astype(jnp.float32)
    ratio = (H3 / H1) ** 2
    table = jnp.concatenate(
        [
            jnp.ones_like(odd1), odd1, odd2, odd3,
            odd1 * odd1, odd2 * odd2, ratio * odd3 * odd3, jnp.zeros_like(odd1),
        ],
        axis=0,
    )
    rest = jnp.zeros((LANES - 8, width), jnp.float32)
    feat[...] = jnp.concatenate([table, rest], axis=0).T.astype(jnp.bfloat16)
    keep_row = (lax.broadcasted_iota(jnp.int32, (8, LANES), 0) == 7).astype(jnp.float32)
    broad = jnp.concatenate([table, keep_row], axis=1)
    wide[...] = jnp.concatenate([broad, broad, broad, jnp.zeros_like(broad)], axis=0).astype(
        jnp.bfloat16
    )
    speeds = []
    for speed in (0.1 * H1 * odd1, (H2 / 30.0) * odd2, (H3 / 30.0) * odd3):
        gain = 0.5 * (1.0 - jnp.abs(speed)) * jnp.where(speed > 0, 1.0, -1.0)
        speeds += [speed, gain]
    cour[...] = jnp.concatenate(speeds + [jnp.zeros_like(odd1)] * 2, axis=0)

    pick = lax.broadcasted_iota(jnp.int32, (nz, LANES), 1) % nz
    pick = (pick == lax.broadcasted_iota(jnp.int32, (nz, LANES), 0)).astype(jnp.bfloat16)
    spread[...] = jnp.dot(
        codes[...].reshape(rows * ny, nz).astype(jnp.float32).astype(jnp.bfloat16),
        pick,
        preferred_element_type=jnp.float32,
    )

    own_line = lax.broadcasted_iota(jnp.int32, (yc, LANES), 0)
    own_line = own_line == lax.broadcasted_iota(jnp.int32, (yc, LANES), 1) // nz
    places = [(x, c) for c in range(chunks) for x in outer_layers]
    places += [(x, c) for x in range(2, rows - 2) for c in range(chunks)]
    for k, (x, c) in enumerate(places):
        row = x * ny + c * yc
        cell_code[k] = jnp.sum(
            jnp.where(own_line, spread[row:row + yc], 0.0), axis=0, keepdims=True
        )

    @pl.when(jnp.logical_not(has_low))
    def _():
        halo_low[...] = jnp.zeros_like(halo_low)

    @pl.when(jnp.logical_not(has_high))
    def _():
        halo_high[...] = jnp.zeros_like(halo_high)

    for copy in load:
        copy.wait()

    def constants(j, dim):
        lanes = pl.ds(pl.multiple_of(j * LANES, LANES), LANES)
        speed = jnp.broadcast_to(cour[2 * dim:2 * dim + 1, lanes], (nz, LANES))
        gain = jnp.broadcast_to(cour[2 * dim + 1:2 * dim + 2, lanes], (nz, LANES))
        return lanes, speed, gain, speed > 0

    def yz_tile(now, layer, index, _):
        x = layer(index // tiles)
        lanes, speed2, gain2, ahead2 = constants(index % tiles, 1)
        _, speed3, gain3, ahead3 = constants(index % tiles, 2)

        cells = [state[now, x, y, :, lanes] for y in range(ny)]
        f_low, f_mid, f, f_up = cells[-2], cells[-1], cells[0], cells[1]
        d = f - f_mid
        l_low = f_mid + gain2 * minmod(f_mid - f_low, d)
        d_up = f_up - f
        l = f + gain2 * minmod(d, d_up)
        change = l - l_low
        for y in range(ny):
            f, f_up, f_next = cells[y], cells[(y + 1) % ny], cells[(y + 2) % ny]
            d_next = f_next - f_up
            l_up = f_up + gain2 * minmod(d_up, d_next)
            change_up = l_up - l
            result = f - speed2 * jnp.where(ahead2, change, change_up)
            dz = pltpu.roll(f, nz - 1, 0) - f
            lz = f + gain3 * minmod(pltpu.roll(dz, 1, 0), dz)
            face = jnp.where(ahead3, lz, pltpu.roll(lz, nz - 1, 0))
            part[x, y, :, lanes] = result - speed3 * (face - pltpu.roll(face, 1, 0))
            d_up = d_next
            l, change = l_up, change_up
        return 0

    def yz(now, layer, count):
        lax.fori_loop(0, count * tiles, functools.partial(yz_tile, now, layer), 0)

    def x_tile(jobs, j, ys):
        lanes, speed, gain, ahead = constants(j, 0)
        for y in ys:
            for sources, outputs in jobs:
                f = [ref[(*lead, y, slice(None), lanes)] for ref, lead in sources]
                d = [b - a for a, b in zip(f[:-1], f[1:])]
                l = [f[i + 1] + gain * minmod(d[i], d[i + 1]) for i in range(len(d) - 1)]
                c = [b - a for a, b in zip(l[:-1], l[1:])]
                for i, x in enumerate(outputs):
                    moved[x, y, :, lanes] = part[x, y, :, lanes] - speed * jnp.where(
                        ahead, c[i], c[i + 1]
                    )

    yu = yc // 2

    def x_inner(now):
        job = ([(state, (now, x)) for x in range(rows)], range(2, rows - 2))

        def tile(index, _):
            x_tile([job], index % tiles, [(index // tiles) * yu + k for k in range(yu)])
            return 0

        lax.fori_loop(0, (ny // yu) * tiles, tile, 0)

    def x_outer(t, now, chunk):
        low = [(halo_low, (t, 0)), (halo_low, (t, 1))] + [(state, (now, x)) for x in range(4)]
        high = [(state, (now, x)) for x in range(rows - 4, rows)] + [
            (halo_high, (t, 0)), (halo_high, (t, 1))
        ]
        jobs = [(low, (0, 1)), (high, (rows - 2, rows - 1))]

        def tile(index, _):
            first = chunk * yc + (index // tiles) * yu
            x_tile(jobs, index % tiles, [first + k for k in range(yu)])
            return 0

        lax.fori_loop(0, (yc // yu) * tiles, tile, 0)

    def block_moments(x, c):
        flat = moved[x, pl.ds(c * yc, yc)].reshape(LANES, width)
        high = flat.astype(jnp.bfloat16)
        low = (flat - high.astype(jnp.float32)).astype(jnp.bfloat16)
        sums = jnp.dot(high, feat[...], preferred_element_type=jnp.float32) + jnp.dot(
            low, feat[...], preferred_element_type=jnp.float32
        )
        return sums.T[0:8]

    def outer_copy(t, c, p):
        return pltpu.make_async_remote_copy(
            src_ref=mom_outer.at[t, mv, c],
            dst_ref=mom_outer.at[t, mv, c],
            send_sem=outer_send.at[t, c, p - 1],
            recv_sem=outer_recv.at[t, c, p - 1],
            device_id={"vert": lax.rem(mv + p, nv)},
            device_id_type=MESH,
        )

    def inner_copy(t, p):
        return pltpu.make_async_remote_copy(
            src_ref=mom_inner.at[t, mv],
            dst_ref=mom_inner.at[t, mv],
            send_sem=inner_send.at[t, p - 1],
            recv_sem=inner_recv.at[t, p - 1],
            device_id={"vert": lax.rem(mv + p, nv)},
            device_id_type=MESH,
        )

    def moments_outer(t, c):
        for i, x in enumerate(outer_layers):
            mom_outer[t, mv, c, i] = block_moments(x, c)
        for p in range(1, nv):
            outer_copy(t, c, p).start()

    def moments_inner(t):
        def layer(i, _):
            for c in range(chunks):
                mom_inner[t, mv, i * chunks + c] = block_moments(i + 2, c)
            return 0

        lax.fori_loop(0, inner_rows, layer, 0)
        for p in range(1, nv):
            inner_copy(t, p).start()

    def coefficients(blocks, first):
        sums = jnp.concatenate(
            [functools.reduce(lambda a, b: a + b, parts) for parts in blocks], axis=1
        )
        count = len(blocks)
        code = jnp.concatenate([cell_code[first + k] for k in range(count)], axis=1)
        weight = sums[0:1]
        density = weight / total
        inverse = 1.0 / weight
        u1 = H1 * sums[1:2] * inverse
        u2 = H2 * sums[2:3] * inverse
        u3 = H3 * sums[3:4] * inverse
        square = (H1 * H1) * (sums[4:5] + sums[5:6] + sums[6:7]) * inverse
        temperature = (square - (u1 * u1 + u2 * u2 + u3 * u3)) / 3.0
        is_inflow = code == 1.0
        is_wall = code == 2.0
        is_open = code == 0.0
        rate = 0.5 * density / (density + knudsen[0:1, 0:1])
        zero = jnp.zeros_like(u1)
        u1 = jnp.where(is_inflow, inflow[0:1, 1:2], jnp.where(is_wall, zero, u1))
        u2 = jnp.where(is_open, u2, zero)
        u3 = jnp.where(is_open, u3, zero)
        temperature = jnp.where(
            is_inflow, inflow[0:1, 2:3], jnp.where(is_wall, inflow[0:1, 3:4], temperature)
        )
        front = jnp.where(
            is_inflow, inflow[0:1, 0:1], jnp.where(is_wall, density, rate * density)
        )
        keep = jnp.where(is_open, 1.0 - rate, zero)
        sharp = (0.5 * LOG2E) / temperature

        def axis_sum(points, spacing, u):
            grid = lax.broadcasted_iota(jnp.int32, (points, count * LANES), 0)
            away = (2.0 * grid.astype(jnp.float32) + (1.0 - points)) * spacing - u
            return jnp.sum(jnp.exp2(-(away * away) * sharp), axis=0, keepdims=True)

        norm = axis_sum(VGX, H1, u1) * axis_sum(VGY, H2, u2) * axis_sum(VGZ, H3, u3)
        constant = jnp.log2(front * total / norm) - (u1 * u1 + u2 * u2 + u3 * u3) * sharp
        slope = 2.0 * sharp
        quad = -(H1 * H1) * sharp
        packed = jnp.concatenate(
            [
                constant, slope * u1 * H1, slope * u2 * H2, slope * u3 * H3,
                quad, quad, quad, keep,
            ],
            axis=0,
        )
        stacked = jnp.concatenate([*split3(packed), jnp.zeros_like(packed)], axis=0)
        for k in range(count):
            coef[first + k] = stacked[:, k * LANES:(k + 1) * LANES].T.astype(jnp.bfloat16)

    def relax_block(then, k, x, c):
        ys = pl.ds(c * yc, yc)
        power = jnp.dot(coef[k], wide[...], preferred_element_type=jnp.float32)
        keep = power[:, width:]
        for j in range(tiles):
            lanes = slice(j * LANES, (j + 1) * LANES)
            old = moved[x, ys, :, lanes]
            new = keep * old.reshape(LANES, LANES) + jnp.exp2(power[:, lanes])
            state[then, x, ys, :, lanes] = new.reshape(old.shape)

    def relax_outer(t, then, c):
        for p in range(1, nv):
            outer_copy(t, c, p).wait_recv()
        coefficients(
            [[mom_outer[t, v, c, i] for v in range(nv)] for i in range(4)], 4 * c
        )
        for i, x in enumerate(outer_layers):
            relax_block(then, 4 * c + i, x, c)

    def relax_inner(t, then):
        for p in range(1, nv):
            inner_copy(t, p).wait_recv()
        coefficients(
            [[mom_inner[t, v, k] for v in range(nv)] for k in range(inner_blocks)], 4 * chunks
        )

        def layer(i, _):
            for c in range(chunks):
                relax_block(then, 4 * chunks + i * chunks + c, i + 2, c)
            return 0

        lax.fori_loop(0, inner_rows, layer, 0)

    final = STEPS % 2

    def write_inner():
        xs = pl.ds(2, inner_rows)
        return pltpu.make_async_copy(state.at[final, xs], out.at[xs], out_sem.at[0])

    def write_outer(c, side):
        xs, ys = pl.ds(side * (rows - 2), 2), pl.ds(c * yc, yc)
        return pltpu.make_async_copy(
            state.at[final, xs, ys], out.at[xs, ys], out_sem.at[1 + 2 * c + side]
        )

    def outer_layer(i):
        return i + inner_rows * (i // 2)

    def step(t, _):
        last = t == STEPS - 1
        now = t % 2
        then = 1 - now
        current = state.at[now]
        following = state.at[then]
        split = inner_rows // 2

        def fill_early():
            yz(now, lambda i: i + 2, split)

        def fill_between():
            yz(now, lambda i: i + 2 + split, inner_rows - split)
            x_inner(now)
            moments_inner(t)

        def fill_late():
            relax_inner(t, then)

        yz(now, outer_layer, 4)
        for c in range(chunks):

            @pl.when(has_high)
            def _():
                to_low(t, c, current).wait_recv()

            @pl.when(has_low)
            def _():
                to_high(t, c, current).wait_recv()

            x_outer(t, now, c)
            moments_outer(t, c)
            if c == 0:
                fill_early()
            if c == chunks - 1:
                fill_late()

            @pl.when(last)
            def _():
                if c == chunks - 1:
                    write_inner().start()

            relax_outer(t, then, c)

            @pl.when(jnp.logical_and(has_low, jnp.logical_not(last)))
            def _():
                to_low(t + 1, c, following).start()

            @pl.when(jnp.logical_and(has_high, jnp.logical_not(last)))
            def _():
                to_high(t + 1, c, following).start()

            @pl.when(last)
            def _():
                for side in range(2):
                    write_outer(c, side).start()

            if c == 0:
                fill_between()

        for c in range(chunks):

            @pl.when(has_low)
            def _():
                to_low(t, c, current).wait_send()

            @pl.when(has_high)
            def _():
                to_high(t, c, current).wait_send()

            for p in range(1, nv):
                outer_copy(t, c, p).wait_send()
        for p in range(1, nv):
            inner_copy(t, p).wait_send()
        return 0

    lax.fori_loop(0, STEPS, step, 0)
    write_inner().wait()
    for c in range(chunks):
        for side in range(2):
            write_outer(c, side).wait()


def body(distribution, velocity_order, cell_codes, knudsen, inflow):
    rows, ny, nz, width = distribution.shape
    nv = lax.axis_size("vert")
    nx_dev = lax.axis_size("gx")
    chunks = ny * nz // LANES
    inner_blocks = (rows - 4) * chunks
    blocks = 4 * chunks + inner_blocks
    hbm = pl.BlockSpec(memory_space=pl.ANY)
    dma = pltpu.SemaphoreType.DMA
    return pl.pallas_call(
        functools.partial(kernel, rows, ny, nz, width, nx_dev, nv),
        out_shape=jax.ShapeDtypeStruct(distribution.shape, jnp.float32),
        in_specs=[pl.BlockSpec(memory_space=pltpu.HBM)] * 5,
        out_specs=hbm,
        scratch_shapes=[
            pltpu.VMEM((2, rows, ny, nz, width), jnp.float32),
            pltpu.VMEM((rows, ny, nz, width), jnp.float32),
            pltpu.VMEM((rows, ny, nz, width), jnp.float32),
            pltpu.VMEM((STEPS, 2, ny, nz, width), jnp.float32),
            pltpu.VMEM((STEPS, 2, ny, nz, width), jnp.float32),
            pltpu.VMEM((STEPS, nv, chunks, 4, 8, LANES), jnp.float32),
            pltpu.VMEM((STEPS, nv, inner_blocks, 8, LANES), jnp.float32),
            pltpu.VMEM((blocks, LANES, 32), jnp.bfloat16),
            pltpu.VMEM((width, LANES), jnp.bfloat16),
            pltpu.VMEM((32, width + LANES), jnp.bfloat16),
            pltpu.VMEM((8, width), jnp.float32),
            pltpu.VMEM((1, width), jnp.int32),
            pltpu.VMEM((rows, ny, nz), jnp.int32),
            pltpu.VMEM((1, 1), jnp.float32),
            pltpu.VMEM((1, 4), jnp.float32),
            pltpu.VMEM((rows * ny, LANES), jnp.float32),
            pltpu.VMEM((blocks, 1, LANES), jnp.float32),
            dma((3,)),
            dma((4,)),
            dma((1 + 2 * chunks,)),
            dma((STEPS, 2, chunks)),
            dma((STEPS, 2, chunks)),
            dma((STEPS, chunks, nv - 1)),
            dma((STEPS, chunks, nv - 1)),
            dma((STEPS, nv - 1)),
            dma((STEPS, nv - 1)),
        ],
        compiler_params=pltpu.CompilerParams(
            collective_id=0, has_side_effects=True, vmem_limit_bytes=48 * 1024 * 1024
        ),
    )(
        distribution,
        velocity_order.reshape(1, width),
        cell_codes,
        knudsen.reshape(1, 1),
        inflow.reshape(1, 4),
    )


def solution(mesh):
    placed = (
        P(("groups", "gx"), None, None, "vert"),
        P("vert"),
        P(("groups", "gx"), None, None),
        P("groups"),
        P("groups"),
    )
    return jax.shard_map(
        body,
        mesh=mesh,
        in_specs=placed,
        out_specs=P(("groups", "gx"), None, None, "vert"),
        check_vma=False,
    )
```

```python
import functools

import jax
import jax.numpy as jnp
from jax import lax
from jax.experimental import pallas as pl
from jax.experimental.pallas import tpu as pltpu
from jax.sharding import PartitionSpec as P

VGX = 16
VGY = 16
VGZ = 8
STEPS = 3
LANES = 128
LOG2E = 1.4426950408889634
MESH = pl.DeviceIdType.MESH

H1 = 3.0 / VGX
H2 = 3.0 / VGY
H3 = 3.0 / VGZ


def minmod(lower, upper):
    return jnp.maximum(jnp.minimum(lower, upper), jnp.minimum(jnp.maximum(lower, upper), 0.0))


def split3(value):
    high = value.astype(jnp.bfloat16).astype(jnp.float32)
    rest = value - high
    middle = rest.astype(jnp.bfloat16).astype(jnp.float32)
    return high, middle, rest - middle


def kernel(
    rows, ny, nz, width, nx_dev, nv,
    dist, order_in, codes_in, knudsen_in, inflow_in,
    out,
    state, part, moved, halo_low, halo_high, mom_outer, mom_inner, coef, feat, wide, cour,
    order, codes, knudsen, inflow, spread, cell_code,
    in_sem, small_sem, out_sem, halo_send, halo_recv,
    outer_send, outer_recv, inner_send, inner_recv,
):
    tiles = width // LANES
    total = float(width * nv)
    yc = LANES // nz
    chunks = ny // yc
    inner_rows = rows - 4
    inner_blocks = inner_rows * chunks
    outer_layers = (0, 1, rows - 2, rows - 1)
    mx = lax.axis_index("gx")
    mv = lax.axis_index("vert")
    has_low = mx > 0
    has_high = mx < nx_dev - 1

    small = [
        pltpu.make_async_copy(source, target, small_sem.at[i])
        for i, (source, target) in enumerate(
            ((order_in, order), (codes_in, codes), (knudsen_in, knudsen), (inflow_in, inflow))
        )
    ]
    for copy in small:
        copy.start()
    load = [
        pltpu.make_async_copy(
            dist.at[pl.ds(first, count)], state.at[0, pl.ds(first, count)], in_sem.at[i]
        )
        for i, (first, count) in enumerate(((0, 2), (rows - 2, 2), (2, inner_rows)))
    ]
    for copy in load:
        copy.start()

    barrier = pltpu.get_barrier_semaphore()

    @pl.when(has_low)
    def _():
        pl.semaphore_signal(barrier, inc=1, device_id={"gx": mx - 1}, device_id_type=MESH)

    @pl.when(has_high)
    def _():
        pl.semaphore_signal(barrier, inc=1, device_id={"gx": mx + 1}, device_id_type=MESH)

    for p in range(1, nv):
        pl.semaphore_signal(
            barrier, inc=1, device_id={"vert": lax.rem(mv + p, nv)}, device_id_type=MESH
        )
    pl.semaphore_wait(
        barrier, nv - 1 + has_low.astype(jnp.int32) + has_high.astype(jnp.int32)
    )

    def to_low(t, c, source):
        ys = pl.ds(c * yc, yc)
        return [
            pltpu.make_async_remote_copy(
                src_ref=source.at[i, ys],
                dst_ref=halo_high.at[t, i, ys],
                send_sem=halo_send.at[t, 0, c, i],
                recv_sem=halo_recv.at[t, 0, c, i],
                device_id={"gx": mx - 1},
                device_id_type=MESH,
            )
            for i in range(2)
        ]

    def to_high(t, c, source):
        ys = pl.ds(c * yc, yc)
        return [
            pltpu.make_async_remote_copy(
                src_ref=source.at[rows - 2 + i, ys],
                dst_ref=halo_low.at[t, i, ys],
                send_sem=halo_send.at[t, 1, c, i],
                recv_sem=halo_recv.at[t, 1, c, i],
                device_id={"gx": mx + 1},
                device_id_type=MESH,
            )
            for i in range(2)
        ]

    crosses_high = mx % 2 == 1

    def send_halo(t, parts, source, allowed):
        def start_high():
            for c in parts:
                for copy in to_high(t, c, source):
                    copy.start()

        @pl.when(jnp.logical_and(allowed, jnp.logical_and(has_high, crosses_high)))
        def _():
            start_high()

        @pl.when(jnp.logical_and(allowed, has_low))
        def _():
            for c in parts:
                for copy in to_low(t, c, source):
                    copy.start()

        @pl.when(
            jnp.logical_and(
                allowed, jnp.logical_and(has_high, jnp.logical_not(crosses_high))
            )
        )
        def _():
            start_high()

    send_halo(0, range(chunks), dist, mx >= 0)

    for copy in small:
        copy.wait()

    slot = order[...]
    odd1 = (2 * (slot // (VGY * VGZ)) + 1 - VGX).astype(jnp.float32)
    odd2 = (2 * ((slot // VGZ) % VGY) + 1 - VGY).astype(jnp.float32)
    odd3 = (2 * (slot % VGZ) + 1 - VGZ).astype(jnp.float32)
    ratio = (H3 / H1) ** 2
    table = jnp.concatenate(
        [
            jnp.ones_like(odd1), odd1, odd2, odd3,
            odd1 * odd1, odd2 * odd2, ratio * odd3 * odd3, jnp.zeros_like(odd1),
        ],
        axis=0,
    )
    rest = jnp.zeros((LANES - 8, width), jnp.float32)
    feat[...] = jnp.concatenate([table, rest], axis=0).T.astype(jnp.bfloat16)
    keep_row = (lax.broadcasted_iota(jnp.int32, (8, LANES), 0) == 7).astype(jnp.float32)
    broad = jnp.concatenate([table, keep_row], axis=1)
    wide[...] = jnp.concatenate([broad, broad, broad, jnp.zeros_like(broad)], axis=0).astype(
        jnp.bfloat16
    )
    speeds = []
    for speed in (0.1 * H1 * odd1, (H2 / 30.0) * odd2, (H3 / 30.0) * odd3):
        gain = 0.5 * (1.0 - jnp.abs(speed)) * jnp.where(speed > 0, 1.0, -1.0)
        speeds += [speed, gain]
    cour[...] = jnp.concatenate(speeds + [jnp.zeros_like(odd1)] * 2, axis=0)

    pick = lax.broadcasted_iota(jnp.int32, (nz, LANES), 1) % nz
    pick = (pick == lax.broadcasted_iota(jnp.int32, (nz, LANES), 0)).astype(jnp.bfloat16)
    spread[...] = jnp.dot(
        codes[...].reshape(rows * ny, nz).astype(jnp.float32).astype(jnp.bfloat16),
        pick,
        preferred_element_type=jnp.float32,
    )

    own_line = lax.broadcasted_iota(jnp.int32, (yc, LANES), 0)
    own_line = own_line == lax.broadcasted_iota(jnp.int32, (yc, LANES), 1) // nz
    places = [(x, c) for c in range(chunks) for x in outer_layers]
    places += [(x, c) for x in range(2, rows - 2) for c in range(chunks)]
    for k, (x, c) in enumerate(places):
        row = x * ny + c * yc
        cell_code[k] = jnp.sum(
            jnp.where(own_line, spread[row:row + yc], 0.0), axis=0, keepdims=True
        )

    @pl.when(jnp.logical_not(has_low))
    def _():
        halo_low[...] = jnp.zeros_like(halo_low)

    @pl.when(jnp.logical_not(has_high))
    def _():
        halo_high[...] = jnp.zeros_like(halo_high)

    for copy in load:
        copy.wait()

    def constants(j, dim):
        lanes = pl.ds(pl.multiple_of(j * LANES, LANES), LANES)
        speed = jnp.broadcast_to(cour[2 * dim:2 * dim + 1, lanes], (nz, LANES))
        gain = jnp.broadcast_to(cour[2 * dim + 1:2 * dim + 2, lanes], (nz, LANES))
        return lanes, speed, gain, speed > 0

    def yz_tile(now, layer, index, _):
        x = layer(index // tiles)
        lanes, speed2, gain2, ahead2 = constants(index % tiles, 1)
        _, speed3, gain3, ahead3 = constants(index % tiles, 2)

        cells = [state[now, x, y, :, lanes] for y in range(ny)]
        f_low, f_mid, f, f_up = cells[-2], cells[-1], cells[0], cells[1]
        d = f - f_mid
        l_low = f_mid + gain2 * minmod(f_mid - f_low, d)
        d_up = f_up - f
        l = f + gain2 * minmod(d, d_up)
        change = l - l_low
        for y in range(ny):
            f, f_up, f_next = cells[y], cells[(y + 1) % ny], cells[(y + 2) % ny]
            d_next = f_next - f_up
            l_up = f_up + gain2 * minmod(d_up, d_next)
            change_up = l_up - l
            result = f - speed2 * jnp.where(ahead2, change, change_up)
            dz = pltpu.roll(f, nz - 1, 0) - f
            lz = f + gain3 * minmod(pltpu.roll(dz, 1, 0), dz)
            face = jnp.where(ahead3, lz, pltpu.roll(lz, nz - 1, 0))
            part[x, y, :, lanes] = result - speed3 * (face - pltpu.roll(face, 1, 0))
            d_up = d_next
            l, change = l_up, change_up
        return 0

    def yz(now, layer, count):
        lax.fori_loop(0, count * tiles, functools.partial(yz_tile, now, layer), 0)

    def x_tile(jobs, j, ys):
        lanes, speed, gain, ahead = constants(j, 0)
        for y in ys:
            for sources, outputs in jobs:
                f = [ref[(*lead, y, slice(None), lanes)] for ref, lead in sources]
                d = [b - a for a, b in zip(f[:-1], f[1:])]
                l = [f[i + 1] + gain * minmod(d[i], d[i + 1]) for i in range(len(d) - 1)]
                c = [b - a for a, b in zip(l[:-1], l[1:])]
                for i, x in enumerate(outputs):
                    moved[x, y, :, lanes] = part[x, y, :, lanes] - speed * jnp.where(
                        ahead, c[i], c[i + 1]
                    )

    yu = yc // 2

    def x_inner(now):
        job = ([(state, (now, x)) for x in range(rows)], range(2, rows - 2))

        def tile(index, _):
            x_tile([job], index % tiles, [(index // tiles) * yu + k for k in range(yu)])
            return 0

        lax.fori_loop(0, (ny // yu) * tiles, tile, 0)

    def x_outer(t, now, chunk):
        low = [(halo_low, (t, 0)), (halo_low, (t, 1))] + [(state, (now, x)) for x in range(4)]
        high = [(state, (now, x)) for x in range(rows - 4, rows)] + [
            (halo_high, (t, 0)), (halo_high, (t, 1))
        ]
        jobs = [(low, (0, 1)), (high, (rows - 2, rows - 1))]

        def tile(index, _):
            first = chunk * yc + (index // tiles) * yu
            x_tile(jobs, index % tiles, [first + k for k in range(yu)])
            return 0

        lax.fori_loop(0, (yc // yu) * tiles, tile, 0)

    def block_moments(x, c):
        flat = moved[x, pl.ds(c * yc, yc)].reshape(LANES, width)
        high = flat.astype(jnp.bfloat16)
        low = (flat - high.astype(jnp.float32)).astype(jnp.bfloat16)
        sums = jnp.dot(high, feat[...], preferred_element_type=jnp.float32) + jnp.dot(
            low, feat[...], preferred_element_type=jnp.float32
        )
        return sums.T[0:8]

    def outer_copy(t, c, p):
        return pltpu.make_async_remote_copy(
            src_ref=mom_outer.at[t, mv, c],
            dst_ref=mom_outer.at[t, mv, c],
            send_sem=outer_send.at[t, c, p - 1],
            recv_sem=outer_recv.at[t, c, p - 1],
            device_id={"vert": lax.rem(mv + p, nv)},
            device_id_type=MESH,
        )

    def inner_copy(t, p):
        return pltpu.make_async_remote_copy(
            src_ref=mom_inner.at[t, mv],
            dst_ref=mom_inner.at[t, mv],
            send_sem=inner_send.at[t, p - 1],
            recv_sem=inner_recv.at[t, p - 1],
            device_id={"vert": lax.rem(mv + p, nv)},
            device_id_type=MESH,
        )

    def moments_outer(t, c):
        for i, x in enumerate(outer_layers):
            mom_outer[t, mv, c, i] = block_moments(x, c)
        for p in range(1, nv):
            outer_copy(t, c, p).start()

    def moments_inner(t):
        def layer(i, _):
            for c in range(chunks):
                mom_inner[t, mv, i * chunks + c] = block_moments(i + 2, c)
            return 0

        lax.fori_loop(0, inner_rows, layer, 0)
        for p in range(1, nv):
            inner_copy(t, p).start()

    def coefficients(blocks, first):
        sums = jnp.concatenate(
            [functools.reduce(lambda a, b: a + b, parts) for parts in blocks], axis=1
        )
        count = len(blocks)
        code = jnp.concatenate([cell_code[first + k] for k in range(count)], axis=1)
        weight = sums[0:1]
        density = weight / total
        inverse = 1.0 / weight
        u1 = H1 * sums[1:2] * inverse
        u2 = H2 * sums[2:3] * inverse
        u3 = H3 * sums[3:4] * inverse
        square = (H1 * H1) * (sums[4:5] + sums[5:6] + sums[6:7]) * inverse
        temperature = (square - (u1 * u1 + u2 * u2 + u3 * u3)) / 3.0
        is_inflow = code == 1.0
        is_wall = code == 2.0
        is_open = code == 0.0
        rate = 0.5 * density / (density + knudsen[0:1, 0:1])
        zero = jnp.zeros_like(u1)
        u1 = jnp.where(is_inflow, inflow[0:1, 1:2], jnp.where(is_wall, zero, u1))
        u2 = jnp.where(is_open, u2, zero)
        u3 = jnp.where(is_open, u3, zero)
        temperature = jnp.where(
            is_inflow, inflow[0:1, 2:3], jnp.where(is_wall, inflow[0:1, 3:4], temperature)
        )
        front = jnp.where(
            is_inflow, inflow[0:1, 0:1], jnp.where(is_wall, density, rate * density)
        )
        keep = jnp.where(is_open, 1.0 - rate, zero)
        sharp = (0.5 * LOG2E) / temperature

        def axis_sum(points, spacing, u):
            grid = lax.broadcasted_iota(jnp.int32, (points, count * LANES), 0)
            away = (2.0 * grid.astype(jnp.float32) + (1.0 - points)) * spacing - u
            return jnp.sum(jnp.exp2(-(away * away) * sharp), axis=0, keepdims=True)

        norm = axis_sum(VGX, H1, u1) * axis_sum(VGY, H2, u2) * axis_sum(VGZ, H3, u3)
        constant = jnp.log2(front * total / norm) - (u1 * u1 + u2 * u2 + u3 * u3) * sharp
        slope = 2.0 * sharp
        quad = -(H1 * H1) * sharp
        packed = jnp.concatenate(
            [
                constant, slope * u1 * H1, slope * u2 * H2, slope * u3 * H3,
                quad, quad, quad, keep,
            ],
            axis=0,
        )
        stacked = jnp.concatenate([*split3(packed), jnp.zeros_like(packed)], axis=0)
        for k in range(count):
            coef[first + k] = stacked[:, k * LANES:(k + 1) * LANES].T.astype(jnp.bfloat16)

    def relax_block(then, k, x, c):
        ys = pl.ds(c * yc, yc)
        power = jnp.dot(coef[k], wide[...], preferred_element_type=jnp.float32)
        keep = power[:, width:]
        for j in range(tiles):
            lanes = slice(j * LANES, (j + 1) * LANES)
            old = moved[x, ys, :, lanes]
            new = keep * old.reshape(LANES, LANES) + jnp.exp2(power[:, lanes])
            state[then, x, ys, :, lanes] = new.reshape(old.shape)

    def relax_outer(t, then, c):
        for p in range(1, nv):
            outer_copy(t, c, p).wait_recv()
        coefficients(
            [[mom_outer[t, v, c, i] for v in range(nv)] for i in range(4)], 4 * c
        )
        for i, x in enumerate(outer_layers):
            relax_block(then, 4 * c + i, x, c)

    def relax_inner(t, then):
        for p in range(1, nv):
            inner_copy(t, p).wait_recv()
        coefficients(
            [[mom_inner[t, v, k] for v in range(nv)] for k in range(inner_blocks)], 4 * chunks
        )

        def layer(i, _):
            for c in range(chunks):
                relax_block(then, 4 * chunks + i * chunks + c, i + 2, c)
            return 0

        lax.fori_loop(0, inner_rows, layer, 0)

    final = STEPS % 2

    def write_inner():
        xs = pl.ds(2, inner_rows)
        return pltpu.make_async_copy(state.at[final, xs], out.at[xs], out_sem.at[0])

    def write_outer(c, side):
        xs, ys = pl.ds(side * (rows - 2), 2), pl.ds(c * yc, yc)
        return pltpu.make_async_copy(
            state.at[final, xs, ys], out.at[xs, ys], out_sem.at[1 + 2 * c + side]
        )

    def outer_layer(i):
        return i + inner_rows * (i // 2)

    def step(t, _):
        last = t == STEPS - 1
        now = t % 2
        then = 1 - now
        current = state.at[now]
        following = state.at[then]
        split = inner_rows // 2

        def fill_early():
            yz(now, lambda i: i + 2, split)

        def fill_between():
            yz(now, lambda i: i + 2 + split, inner_rows - split)
            x_inner(now)
            moments_inner(t)

        def fill_late():
            relax_inner(t, then)

        yz(now, outer_layer, 4)
        for c in range(chunks):

            @pl.when(has_high)
            def _():
                for copy in to_low(t, c, current):
                    copy.wait_recv()

            @pl.when(has_low)
            def _():
                for copy in to_high(t, c, current):
                    copy.wait_recv()

            x_outer(t, now, c)
            moments_outer(t, c)
            if c == 0:
                fill_early()
            if c == chunks - 1:
                fill_late()

            @pl.when(last)
            def _():
                if c == chunks - 1:
                    write_inner().start()

            relax_outer(t, then, c)

            send_halo(t + 1, [c], following, jnp.logical_not(last))

            @pl.when(last)
            def _():
                for side in range(2):
                    write_outer(c, side).start()

            if c == 0:
                fill_between()

        for c in range(chunks):

            @pl.when(has_low)
            def _():
                for copy in to_low(t, c, current):
                    copy.wait_send()

            @pl.when(has_high)
            def _():
                for copy in to_high(t, c, current):
                    copy.wait_send()

            for p in range(1, nv):
                outer_copy(t, c, p).wait_send()
        for p in range(1, nv):
            inner_copy(t, p).wait_send()
        return 0

    lax.fori_loop(0, STEPS, step, 0)
    write_inner().wait()
    for c in range(chunks):
        for side in range(2):
            write_outer(c, side).wait()


def body(distribution, velocity_order, cell_codes, knudsen, inflow):
    rows, ny, nz, width = distribution.shape
    nv = lax.axis_size("vert")
    nx_dev = lax.axis_size("gx")
    chunks = ny * nz // LANES
    inner_blocks = (rows - 4) * chunks
    blocks = 4 * chunks + inner_blocks
    hbm = pl.BlockSpec(memory_space=pl.ANY)
    dma = pltpu.SemaphoreType.DMA
    return pl.pallas_call(
        functools.partial(kernel, rows, ny, nz, width, nx_dev, nv),
        out_shape=jax.ShapeDtypeStruct(distribution.shape, jnp.float32),
        in_specs=[pl.BlockSpec(memory_space=pltpu.HBM)] * 5,
        out_specs=hbm,
        scratch_shapes=[
            pltpu.VMEM((2, rows, ny, nz, width), jnp.float32),
            pltpu.VMEM((rows, ny, nz, width), jnp.float32),
            pltpu.VMEM((rows, ny, nz, width), jnp.float32),
            pltpu.VMEM((STEPS, 2, ny, nz, width), jnp.float32),
            pltpu.VMEM((STEPS, 2, ny, nz, width), jnp.float32),
            pltpu.VMEM((STEPS, nv, chunks, 4, 8, LANES), jnp.float32),
            pltpu.VMEM((STEPS, nv, inner_blocks, 8, LANES), jnp.float32),
            pltpu.VMEM((blocks, LANES, 32), jnp.bfloat16),
            pltpu.VMEM((width, LANES), jnp.bfloat16),
            pltpu.VMEM((32, width + LANES), jnp.bfloat16),
            pltpu.VMEM((8, width), jnp.float32),
            pltpu.VMEM((1, width), jnp.int32),
            pltpu.VMEM((rows, ny, nz), jnp.int32),
            pltpu.VMEM((1, 1), jnp.float32),
            pltpu.VMEM((1, 4), jnp.float32),
            pltpu.VMEM((rows * ny, LANES), jnp.float32),
            pltpu.VMEM((blocks, 1, LANES), jnp.float32),
            dma((3,)),
            dma((4,)),
            dma((1 + 2 * chunks,)),
            dma((STEPS, 2, chunks, 2)),
            dma((STEPS, 2, chunks, 2)),
            dma((STEPS, chunks, nv - 1)),
            dma((STEPS, chunks, nv - 1)),
            dma((STEPS, nv - 1)),
            dma((STEPS, nv - 1)),
        ],
        compiler_params=pltpu.CompilerParams(
            collective_id=0, has_side_effects=True, vmem_limit_bytes=62 * 1024 * 1024
        ),
    )(
        distribution,
        velocity_order.reshape(1, width),
        cell_codes,
        knudsen.reshape(1, 1),
        inflow.reshape(1, 4),
    )


def solution(mesh):
    placed = (
        P(("groups", "gx"), None, None, "vert"),
        P("vert"),
        P(("groups", "gx"), None, None),
        P("groups"),
        P("groups"),
    )
    return jax.shard_map(
        body,
        mesh=mesh,
        in_specs=placed,
        out_specs=P(("groups", "gx"), None, None, "vert"),
        check_vma=False,
    )
```

```python
import functools

import jax
import jax.numpy as jnp
from jax import lax
from jax.experimental import pallas as pl
from jax.experimental.pallas import tpu as pltpu
from jax.sharding import PartitionSpec as P

VGX = 16
VGY = 16
VGZ = 8
STEPS = 3
LANES = 128
LOG2E = 1.4426950408889634
MESH = pl.DeviceIdType.MESH

H1 = 3.0 / VGX
H2 = 3.0 / VGY
H3 = 3.0 / VGZ


def minmod(lower, upper):
    return jnp.maximum(jnp.minimum(lower, upper), jnp.minimum(jnp.maximum(lower, upper), 0.0))


def split3(value):
    high = value.astype(jnp.bfloat16).astype(jnp.float32)
    rest = value - high
    middle = rest.astype(jnp.bfloat16).astype(jnp.float32)
    return high, middle, rest - middle


def kernel(
    rows, ny, nz, width, nx_dev, nv,
    dist, scalars_in, codes_in,
    out,
    state, part, moved, halo_low, halo_high, mom_outer, mom_inner, coef, feat, wide, cour,
    scalars, codes, spread, cell_code,
    in_sem, small_sem, out_sem, halo_send, halo_recv,
    outer_send, outer_recv, inner_send, inner_recv,
):
    tiles = width // LANES
    total = float(width * nv)
    yc = LANES // nz
    chunks = ny // yc
    inner_rows = rows - 4
    inner_blocks = inner_rows * chunks
    outer_layers = (0, 1, rows - 2, rows - 1)
    mx = lax.axis_index("gx")
    mv = lax.axis_index("vert")
    has_low = mx > 0
    has_high = mx < nx_dev - 1

    small = [
        pltpu.make_async_copy(source, target, small_sem.at[i])
        for i, (source, target) in enumerate(
            ((scalars_in, scalars), (codes_in, codes))
        )
    ]
    for copy in small:
        copy.start()
    load = [
        pltpu.make_async_copy(
            dist.at[pl.ds(first, count)], state.at[0, pl.ds(first, count)], in_sem.at[i]
        )
        for i, (first, count) in enumerate(((0, 2), (rows - 2, 2), (2, inner_rows)))
    ]
    for copy in load:
        copy.start()

    barrier = pltpu.get_barrier_semaphore()

    @pl.when(has_low)
    def _():
        pl.semaphore_signal(barrier, inc=1, device_id={"gx": mx - 1}, device_id_type=MESH)

    @pl.when(has_high)
    def _():
        pl.semaphore_signal(barrier, inc=1, device_id={"gx": mx + 1}, device_id_type=MESH)

    for p in range(1, nv):
        pl.semaphore_signal(
            barrier, inc=1, device_id={"vert": lax.rem(mv + p, nv)}, device_id_type=MESH
        )
    pl.semaphore_wait(
        barrier, nv - 1 + has_low.astype(jnp.int32) + has_high.astype(jnp.int32)
    )

    def to_low(t, c, source):
        ys = pl.ds(c * yc, yc)
        return [
            pltpu.make_async_remote_copy(
                src_ref=source.at[i, ys],
                dst_ref=halo_high.at[t, i, ys],
                send_sem=halo_send.at[t, 0, c, i],
                recv_sem=halo_recv.at[t, 0, c, i],
                device_id={"gx": mx - 1},
                device_id_type=MESH,
            )
            for i in range(2)
        ]

    def to_high(t, c, source):
        ys = pl.ds(c * yc, yc)
        return [
            pltpu.make_async_remote_copy(
                src_ref=source.at[rows - 2 + i, ys],
                dst_ref=halo_low.at[t, i, ys],
                send_sem=halo_send.at[t, 1, c, i],
                recv_sem=halo_recv.at[t, 1, c, i],
                device_id={"gx": mx + 1},
                device_id_type=MESH,
            )
            for i in range(2)
        ]

    crosses_high = mx % 2 == 1

    def send_halo(t, parts, source, allowed):
        def start_high():
            for c in parts:
                for copy in to_high(t, c, source):
                    copy.start()

        @pl.when(jnp.logical_and(allowed, jnp.logical_and(has_high, crosses_high)))
        def _():
            start_high()

        @pl.when(jnp.logical_and(allowed, has_low))
        def _():
            for c in parts:
                for copy in to_low(t, c, source):
                    copy.start()

        @pl.when(
            jnp.logical_and(
                allowed, jnp.logical_and(has_high, jnp.logical_not(crosses_high))
            )
        )
        def _():
            start_high()

    send_halo(0, range(chunks), dist, mx >= 0)

    for copy in small:
        copy.wait()

    slot = scalars[:, :width].astype(jnp.int32)
    inflow = scalars[:, width:width + 4]
    knudsen = scalars[:, width + 4:width + 5]
    odd1 = (2 * (slot // (VGY * VGZ)) + 1 - VGX).astype(jnp.float32)
    odd2 = (2 * ((slot // VGZ) % VGY) + 1 - VGY).astype(jnp.float32)
    odd3 = (2 * (slot % VGZ) + 1 - VGZ).astype(jnp.float32)
    ratio = (H3 / H1) ** 2
    table = jnp.concatenate(
        [
            jnp.ones_like(odd1), odd1, odd2, odd3,
            odd1 * odd1, odd2 * odd2, ratio * odd3 * odd3, jnp.zeros_like(odd1),
        ],
        axis=0,
    )
    rest = jnp.zeros((LANES - 8, width), jnp.float32)
    feat[...] = jnp.concatenate([table, rest], axis=0).T.astype(jnp.bfloat16)
    keep_row = (lax.broadcasted_iota(jnp.int32, (8, LANES), 0) == 7).astype(jnp.float32)
    broad = jnp.concatenate([table, keep_row], axis=1)
    wide[...] = jnp.concatenate([broad, broad, broad, jnp.zeros_like(broad)], axis=0).astype(
        jnp.bfloat16
    )
    speeds = []
    for speed in (0.1 * H1 * odd1, (H2 / 30.0) * odd2, (H3 / 30.0) * odd3):
        gain = 0.5 * (1.0 - jnp.abs(speed)) * jnp.where(speed > 0, 1.0, -1.0)
        speeds += [speed, gain]
    cour[...] = jnp.concatenate(speeds + [jnp.zeros_like(odd1)] * 2, axis=0)

    pick = lax.broadcasted_iota(jnp.int32, (nz, LANES), 1) % nz
    pick = (pick == lax.broadcasted_iota(jnp.int32, (nz, LANES), 0)).astype(jnp.bfloat16)
    spread[...] = jnp.dot(
        codes[...].reshape(rows * ny, nz).astype(jnp.float32).astype(jnp.bfloat16),
        pick,
        preferred_element_type=jnp.float32,
    )

    own_line = lax.broadcasted_iota(jnp.int32, (yc, LANES), 0)
    own_line = own_line == lax.broadcasted_iota(jnp.int32, (yc, LANES), 1) // nz
    places = [(x, c) for c in range(chunks) for x in outer_layers]
    places += [(x, c) for x in range(2, rows - 2) for c in range(chunks)]
    for k, (x, c) in enumerate(places):
        row = x * ny + c * yc
        cell_code[k] = jnp.sum(
            jnp.where(own_line, spread[row:row + yc], 0.0), axis=0, keepdims=True
        )

    @pl.when(jnp.logical_not(has_low))
    def _():
        halo_low[...] = jnp.zeros_like(halo_low)

    @pl.when(jnp.logical_not(has_high))
    def _():
        halo_high[...] = jnp.zeros_like(halo_high)

    for copy in load:
        copy.wait()

    def constants(j, dim):
        lanes = pl.ds(pl.multiple_of(j * LANES, LANES), LANES)
        speed = jnp.broadcast_to(cour[2 * dim:2 * dim + 1, lanes], (nz, LANES))
        gain = jnp.broadcast_to(cour[2 * dim + 1:2 * dim + 2, lanes], (nz, LANES))
        return lanes, speed, gain, speed > 0

    def yz_tile(now, layer, index, _):
        x = layer(index // tiles)
        lanes, speed2, gain2, ahead2 = constants(index % tiles, 1)
        _, speed3, gain3, ahead3 = constants(index % tiles, 2)

        cells = [state[now, x, y, :, lanes] for y in range(ny)]
        f_low, f_mid, f, f_up = cells[-2], cells[-1], cells[0], cells[1]
        d = f - f_mid
        l_low = f_mid + gain2 * minmod(f_mid - f_low, d)
        d_up = f_up - f
        l = f + gain2 * minmod(d, d_up)
        change = l - l_low
        for y in range(ny):
            f, f_up, f_next = cells[y], cells[(y + 1) % ny], cells[(y + 2) % ny]
            d_next = f_next - f_up
            l_up = f_up + gain2 * minmod(d_up, d_next)
            change_up = l_up - l
            result = f - speed2 * jnp.where(ahead2, change, change_up)
            dz = pltpu.roll(f, nz - 1, 0) - f
            lz = f + gain3 * minmod(pltpu.roll(dz, 1, 0), dz)
            face = jnp.where(ahead3, lz, pltpu.roll(lz, nz - 1, 0))
            part[x, y, :, lanes] = result - speed3 * (face - pltpu.roll(face, 1, 0))
            d_up = d_next
            l, change = l_up, change_up
        return 0

    def yz(now, layer, count):
        lax.fori_loop(0, count * tiles, functools.partial(yz_tile, now, layer), 0)

    def x_tile(jobs, j, ys):
        lanes, speed, gain, ahead = constants(j, 0)
        for y in ys:
            for sources, outputs in jobs:
                f = [ref[(*lead, y, slice(None), lanes)] for ref, lead in sources]
                d = [b - a for a, b in zip(f[:-1], f[1:])]
                l = [f[i + 1] + gain * minmod(d[i], d[i + 1]) for i in range(len(d) - 1)]
                c = [b - a for a, b in zip(l[:-1], l[1:])]
                for i, x in enumerate(outputs):
                    moved[x, y, :, lanes] = part[x, y, :, lanes] - speed * jnp.where(
                        ahead, c[i], c[i + 1]
                    )

    yu = yc // 2

    def x_inner(now):
        job = ([(state, (now, x)) for x in range(rows)], range(2, rows - 2))

        def tile(index, _):
            x_tile([job], index % tiles, [(index // tiles) * yu + k for k in range(yu)])
            return 0

        lax.fori_loop(0, (ny // yu) * tiles, tile, 0)

    def x_outer(t, now, chunk):
        low = [(halo_low, (t, 0)), (halo_low, (t, 1))] + [(state, (now, x)) for x in range(4)]
        high = [(state, (now, x)) for x in range(rows - 4, rows)] + [
            (halo_high, (t, 0)), (halo_high, (t, 1))
        ]
        jobs = [(low, (0, 1)), (high, (rows - 2, rows - 1))]

        def tile(index, _):
            first = chunk * yc + (index // tiles) * yu
            x_tile(jobs, index % tiles, [first + k for k in range(yu)])
            return 0

        lax.fori_loop(0, (yc // yu) * tiles, tile, 0)

    def block_moments(places):
        flat = jnp.concatenate(
            [moved[x, pl.ds(c * yc, yc)].reshape(LANES, width) for x, c in places], axis=0
        )
        high = flat.astype(jnp.bfloat16)
        low = (flat - high.astype(jnp.float32)).astype(jnp.bfloat16)
        sums = jnp.dot(
            jnp.concatenate([high, low], axis=0), feat[...], preferred_element_type=jnp.float32
        )
        count = len(places) * LANES
        sums = sums[:count] + sums[count:]
        return [sums[k * LANES:(k + 1) * LANES].T[0:8] for k in range(len(places))]

    def outer_copy(t, c, p):
        return pltpu.make_async_remote_copy(
            src_ref=mom_outer.at[t, mv, c],
            dst_ref=mom_outer.at[t, mv, c],
            send_sem=outer_send.at[t, c, p - 1],
            recv_sem=outer_recv.at[t, c, p - 1],
            device_id={"vert": lax.rem(mv + p, nv)},
            device_id_type=MESH,
        )

    def inner_copy(t, p):
        return pltpu.make_async_remote_copy(
            src_ref=mom_inner.at[t, mv],
            dst_ref=mom_inner.at[t, mv],
            send_sem=inner_send.at[t, p - 1],
            recv_sem=inner_recv.at[t, p - 1],
            device_id={"vert": lax.rem(mv + p, nv)},
            device_id_type=MESH,
        )

    def moments_outer(t, c):
        for i, sums in enumerate(block_moments([(x, c) for x in outer_layers])):
            mom_outer[t, mv, c, i] = sums
        for p in range(1, nv):
            outer_copy(t, c, p).start()

    def moments_inner(t):
        def layer(i, _):
            for c, sums in enumerate(block_moments([(i + 2, c) for c in range(chunks)])):
                mom_inner[t, mv, i * chunks + c] = sums
            return 0

        lax.fori_loop(0, inner_rows, layer, 0)
        for p in range(1, nv):
            inner_copy(t, p).start()

    def coefficients(blocks, first):
        sums = jnp.concatenate(
            [functools.reduce(lambda a, b: a + b, parts) for parts in blocks], axis=1
        )
        count = len(blocks)
        code = jnp.concatenate([cell_code[first + k] for k in range(count)], axis=1)
        weight = sums[0:1]
        density = weight / total
        inverse = 1.0 / weight
        u1 = H1 * sums[1:2] * inverse
        u2 = H2 * sums[2:3] * inverse
        u3 = H3 * sums[3:4] * inverse
        square = (H1 * H1) * (sums[4:5] + sums[5:6] + sums[6:7]) * inverse
        temperature = (square - (u1 * u1 + u2 * u2 + u3 * u3)) / 3.0
        is_inflow = code == 1.0
        is_wall = code == 2.0
        is_open = code == 0.0
        rate = 0.5 * density / (density + knudsen)
        zero = jnp.zeros_like(u1)
        u1 = jnp.where(is_inflow, inflow[0:1, 1:2], jnp.where(is_wall, zero, u1))
        u2 = jnp.where(is_open, u2, zero)
        u3 = jnp.where(is_open, u3, zero)
        temperature = jnp.where(
            is_inflow, inflow[0:1, 2:3], jnp.where(is_wall, inflow[0:1, 3:4], temperature)
        )
        front = jnp.where(
            is_inflow, inflow[0:1, 0:1], jnp.where(is_wall, density, rate * density)
        )
        keep = jnp.where(is_open, 1.0 - rate, zero)
        sharp = (0.5 * LOG2E) / temperature

        def axis_sum(points, spacing, u):
            grid = lax.broadcasted_iota(jnp.int32, (points, count * LANES), 0)
            away = (2.0 * grid.astype(jnp.float32) + (1.0 - points)) * spacing - u
            return jnp.sum(jnp.exp2(-(away * away) * sharp), axis=0, keepdims=True)

        norm = axis_sum(VGX, H1, u1) * axis_sum(VGY, H2, u2) * axis_sum(VGZ, H3, u3)
        constant = jnp.log2(front * total / norm) - (u1 * u1 + u2 * u2 + u3 * u3) * sharp
        slope = 2.0 * sharp
        quad = -(H1 * H1) * sharp
        packed = jnp.concatenate(
            [
                constant, slope * u1 * H1, slope * u2 * H2, slope * u3 * H3,
                quad, quad, quad, keep,
            ],
            axis=0,
        )
        stacked = jnp.concatenate([*split3(packed), jnp.zeros_like(packed)], axis=0)
        for k in range(count):
            coef[first + k] = stacked[:, k * LANES:(k + 1) * LANES].T.astype(jnp.bfloat16)

    def relax_blocks(then, first, places):
        count = len(places)
        power = jnp.dot(
            coef[pl.ds(first, count)].reshape(count * LANES, 32),
            wide[...],
            preferred_element_type=jnp.float32,
        )
        for k, (x, c) in enumerate(places):
            cells = slice(k * LANES, (k + 1) * LANES)
            ys = pl.ds(c * yc, yc)
            keep = power[cells, width:]
            for j in range(tiles):
                lanes = slice(j * LANES, (j + 1) * LANES)
                old = moved[x, ys, :, lanes]
                new = keep * old.reshape(LANES, LANES) + jnp.exp2(power[cells, lanes])
                state[then, x, ys, :, lanes] = new.reshape(old.shape)

    def relax_outer(t, then, c):
        for p in range(1, nv):
            outer_copy(t, c, p).wait_recv()
        coefficients(
            [[mom_outer[t, v, c, i] for v in range(nv)] for i in range(4)], 4 * c
        )
        relax_blocks(then, 4 * c, [(x, c) for x in outer_layers])

    def prepare_inner(t):
        for p in range(1, nv):
            inner_copy(t, p).wait_recv()
        coefficients(
            [[mom_inner[t, v, k] for v in range(nv)] for k in range(inner_blocks)], 4 * chunks
        )

    def relax_inner(then, first, count):
        def layer(i, _):
            relax_blocks(
                then, 4 * chunks + i * chunks, [(i + 2, c) for c in range(chunks)]
            )
            return 0

        lax.fori_loop(first, first + count, layer, 0)

    final = STEPS % 2

    def write_inner():
        xs = pl.ds(2, inner_rows)
        return pltpu.make_async_copy(state.at[final, xs], out.at[xs], out_sem.at[0])

    def write_outer(c, side):
        xs, ys = pl.ds(side * (rows - 2), 2), pl.ds(c * yc, yc)
        return pltpu.make_async_copy(
            state.at[final, xs, ys], out.at[xs, ys], out_sem.at[1 + 2 * c + side]
        )

    def outer_layer(i):
        return i + inner_rows * (i // 2)

    def step(t, _):
        last = t == STEPS - 1
        now = t % 2
        then = 1 - now
        current = state.at[now]
        following = state.at[then]
        split = inner_rows // 2

        def fill_early():
            yz(now, lambda i: i + 2, split)

        def fill_between():
            yz(now, lambda i: i + 2 + split, inner_rows - split)
            x_inner(now)
            moments_inner(t)

        def fill_late():
            prepare_inner(t)
            relax_inner(then, 0, split)

        yz(now, outer_layer, 4)
        for c in range(chunks):

            @pl.when(has_high)
            def _():
                for copy in to_low(t, c, current):
                    copy.wait_recv()

            @pl.when(has_low)
            def _():
                for copy in to_high(t, c, current):
                    copy.wait_recv()

            x_outer(t, now, c)
            moments_outer(t, c)
            if c == 0:
                fill_early()
            if c == chunks - 1:
                fill_late()

            relax_outer(t, then, c)

            send_halo(t + 1, [c], following, jnp.logical_not(last))

            @pl.when(last)
            def _():
                for side in range(2):
                    write_outer(c, side).start()

            if c == 0:
                fill_between()
            if c == chunks - 1:
                relax_inner(then, split, inner_rows - split)

                @pl.when(last)
                def _():
                    write_inner().start()

        for c in range(chunks):

            @pl.when(has_low)
            def _():
                for copy in to_low(t, c, current):
                    copy.wait_send()

            @pl.when(has_high)
            def _():
                for copy in to_high(t, c, current):
                    copy.wait_send()

            for p in range(1, nv):
                outer_copy(t, c, p).wait_send()
        for p in range(1, nv):
            inner_copy(t, p).wait_send()
        return 0

    lax.fori_loop(0, STEPS, step, 0)
    write_inner().wait()
    for c in range(chunks):
        for side in range(2):
            write_outer(c, side).wait()


def body(distribution, velocity_order, cell_codes, knudsen, inflow):
    rows, ny, nz, width = distribution.shape
    nv = lax.axis_size("vert")
    nx_dev = lax.axis_size("gx")
    chunks = ny * nz // LANES
    inner_blocks = (rows - 4) * chunks
    blocks = 4 * chunks + inner_blocks
    scalars = jnp.concatenate(
        [
            velocity_order.astype(jnp.float32),
            inflow,
            knudsen,
            jnp.zeros((LANES - 5,), jnp.float32),
        ]
    )
    hbm = pl.BlockSpec(memory_space=pl.ANY)
    dma = pltpu.SemaphoreType.DMA
    return pl.pallas_call(
        functools.partial(kernel, rows, ny, nz, width, nx_dev, nv),
        out_shape=jax.ShapeDtypeStruct(distribution.shape, jnp.float32),
        in_specs=[hbm] * 3,
        out_specs=hbm,
        scratch_shapes=[
            pltpu.VMEM((2, rows, ny, nz, width), jnp.float32),
            pltpu.VMEM((rows, ny, nz, width), jnp.float32),
            pltpu.VMEM((rows, ny, nz, width), jnp.float32),
            pltpu.VMEM((STEPS, 2, ny, nz, width), jnp.float32),
            pltpu.VMEM((STEPS, 2, ny, nz, width), jnp.float32),
            pltpu.VMEM((STEPS, nv, chunks, 4, 8, LANES), jnp.float32),
            pltpu.VMEM((STEPS, nv, inner_blocks, 8, LANES), jnp.float32),
            pltpu.VMEM((blocks, LANES, 32), jnp.bfloat16),
            pltpu.VMEM((width, LANES), jnp.bfloat16),
            pltpu.VMEM((32, width + LANES), jnp.bfloat16),
            pltpu.VMEM((8, width), jnp.float32),
            pltpu.VMEM((1, width + LANES), jnp.float32),
            pltpu.VMEM((rows, ny, nz), jnp.int32),
            pltpu.VMEM((rows * ny, LANES), jnp.float32),
            pltpu.VMEM((blocks, 1, LANES), jnp.float32),
            dma((3,)),
            dma((2,)),
            dma((1 + 2 * chunks,)),
            dma((STEPS, 2, chunks, 2)),
            dma((STEPS, 2, chunks, 2)),
            dma((STEPS, chunks, nv - 1)),
            dma((STEPS, chunks, nv - 1)),
            dma((STEPS, nv - 1)),
            dma((STEPS, nv - 1)),
        ],
        compiler_params=pltpu.CompilerParams(
            collective_id=0, has_side_effects=True, vmem_limit_bytes=48 * 1024 * 1024
        ),
    )(
        distribution,
        scalars.reshape(1, -1),
        cell_codes,
    )


def solution(mesh):
    placed = (
        P(("groups", "gx"), None, None, "vert"),
        P("vert"),
        P(("groups", "gx"), None, None),
        P("groups"),
        P("groups"),
    )
    return jax.shard_map(
        body,
        mesh=mesh,
        in_specs=placed,
        out_specs=P(("groups", "gx"), None, None, "vert"),
        check_vma=False,
    )
```

```python
import functools

import jax
import jax.numpy as jnp
from jax import lax
from jax.experimental import pallas as pl
from jax.experimental.pallas import tpu as pltpu
from jax.sharding import PartitionSpec as P

VGX = 16
VGY = 16
VGZ = 8
STEPS = 3
LANES = 128
LOG2E = 1.4426950408889634
MESH = pl.DeviceIdType.MESH

H1 = 3.0 / VGX
H2 = 3.0 / VGY
H3 = 3.0 / VGZ


def minmod(lower, upper):
    return jnp.maximum(jnp.minimum(lower, upper), jnp.minimum(jnp.maximum(lower, upper), 0.0))


def split3(value):
    high = value.astype(jnp.bfloat16).astype(jnp.float32)
    rest = value - high
    middle = rest.astype(jnp.bfloat16).astype(jnp.float32)
    return high, middle, rest - middle


def kernel(
    rows, ny, nz, width, nx_dev, nv,
    dist, order_in, codes_in, knudsen_in, inflow_in,
    out,
    state, part, moved, halo_low, halo_high, mom_outer, mom_inner, coef, feat, wide, cour,
    order, codes, knudsen, inflow, spread, cell_code,
    in_sem, small_sem, out_sem, halo_send, halo_recv,
    outer_send, outer_recv, inner_send, inner_recv,
):
    tiles = width // LANES
    total = float(width * nv)
    yc = LANES // nz
    chunks = ny // yc
    inner_rows = rows - 4
    inner_blocks = inner_rows * chunks
    outer_layers = (0, 1, rows - 2, rows - 1)
    mx = lax.axis_index("gx")
    mv = lax.axis_index("vert")
    has_low = mx > 0
    has_high = mx < nx_dev - 1

    small = [
        pltpu.make_async_copy(source, target, small_sem.at[i])
        for i, (source, target) in enumerate(
            ((order_in, order), (codes_in, codes), (knudsen_in, knudsen), (inflow_in, inflow))
        )
    ]
    for copy in small:
        copy.start()
    load = [
        pltpu.make_async_copy(
            dist.at[pl.ds(first, count)], state.at[0, pl.ds(first, count)], in_sem.at[i]
        )
        for i, (first, count) in enumerate(((0, 2), (rows - 2, 2), (2, inner_rows)))
    ]
    for copy in load:
        copy.start()

    barrier = pltpu.get_barrier_semaphore()

    @pl.when(has_low)
    def _():
        pl.semaphore_signal(barrier, inc=1, device_id={"gx": mx - 1}, device_id_type=MESH)

    @pl.when(has_high)
    def _():
        pl.semaphore_signal(barrier, inc=1, device_id={"gx": mx + 1}, device_id_type=MESH)

    for p in range(1, nv):
        pl.semaphore_signal(
            barrier, inc=1, device_id={"vert": lax.rem(mv + p, nv)}, device_id_type=MESH
        )
    pl.semaphore_wait(
        barrier, nv - 1 + has_low.astype(jnp.int32) + has_high.astype(jnp.int32)
    )

    def to_low(t, c, source):
        ys = pl.ds(c * yc, yc)
        return pltpu.make_async_remote_copy(
            src_ref=source.at[pl.ds(0, 2), ys],
            dst_ref=halo_high.at[t, :, ys],
            send_sem=halo_send.at[t, 0, c],
            recv_sem=halo_recv.at[t, 0, c],
            device_id={"gx": mx - 1},
            device_id_type=MESH,
        )

    def to_high(t, c, source):
        ys = pl.ds(c * yc, yc)
        return pltpu.make_async_remote_copy(
            src_ref=source.at[pl.ds(rows - 2, 2), ys],
            dst_ref=halo_low.at[t, :, ys],
            send_sem=halo_send.at[t, 1, c],
            recv_sem=halo_recv.at[t, 1, c],
            device_id={"gx": mx + 1},
            device_id_type=MESH,
        )

    @pl.when(has_low)
    def _():
        for c in range(chunks):
            to_low(0, c, dist).start()

    @pl.when(has_high)
    def _():
        for c in range(chunks):
            to_high(0, c, dist).start()

    for copy in small:
        copy.wait()

    slot = order[...]
    odd1 = (2 * (slot // (VGY * VGZ)) + 1 - VGX).astype(jnp.float32)
    odd2 = (2 * ((slot // VGZ) % VGY) + 1 - VGY).astype(jnp.float32)
    odd3 = (2 * (slot % VGZ) + 1 - VGZ).astype(jnp.float32)
    ratio = (H3 / H1) ** 2
    table = jnp.concatenate(
        [
            jnp.ones_like(odd1), odd1, odd2, odd3,
            odd1 * odd1, odd2 * odd2, ratio * odd3 * odd3, jnp.zeros_like(odd1),
        ],
        axis=0,
    )
    rest = jnp.zeros((LANES - 8, width), jnp.float32)
    feat[...] = jnp.concatenate([table, rest], axis=0).T.astype(jnp.bfloat16)
    keep_row = (lax.broadcasted_iota(jnp.int32, (8, LANES), 0) == 7).astype(jnp.float32)
    broad = jnp.concatenate([table, keep_row], axis=1)
    wide[...] = jnp.concatenate([broad, broad, broad, jnp.zeros_like(broad)], axis=0).astype(
        jnp.bfloat16
    )
    speeds = []
    for speed in (0.1 * H1 * odd1, (H2 / 30.0) * odd2, (H3 / 30.0) * odd3):
        gain = 0.5 * (1.0 - jnp.abs(speed)) * jnp.where(speed > 0, 1.0, -1.0)
        speeds += [speed, gain]
    cour[...] = jnp.concatenate(speeds + [jnp.zeros_like(odd1)] * 2, axis=0)

    pick = lax.broadcasted_iota(jnp.int32, (nz, LANES), 1) % nz
    pick = (pick == lax.broadcasted_iota(jnp.int32, (nz, LANES), 0)).astype(jnp.bfloat16)
    spread[...] = jnp.dot(
        codes[...].reshape(rows * ny, nz).astype(jnp.float32).astype(jnp.bfloat16),
        pick,
        preferred_element_type=jnp.float32,
    )

    own_line = lax.broadcasted_iota(jnp.int32, (yc, LANES), 0)
    own_line = own_line == lax.broadcasted_iota(jnp.int32, (yc, LANES), 1) // nz
    places = [(x, c) for c in range(chunks) for x in outer_layers]
    places += [(x, c) for x in range(2, rows - 2) for c in range(chunks)]
    for k, (x, c) in enumerate(places):
        row = x * ny + c * yc
        cell_code[k] = jnp.sum(
            jnp.where(own_line, spread[row:row + yc], 0.0), axis=0, keepdims=True
        )

    @pl.when(jnp.logical_not(has_low))
    def _():
        halo_low[...] = jnp.zeros_like(halo_low)

    @pl.when(jnp.logical_not(has_high))
    def _():
        halo_high[...] = jnp.zeros_like(halo_high)

    for copy in load:
        copy.wait()

    def constants(j, dim):
        lanes = pl.ds(pl.multiple_of(j * LANES, LANES), LANES)
        speed = jnp.broadcast_to(cour[2 * dim:2 * dim + 1, lanes], (nz, LANES))
        gain = jnp.broadcast_to(cour[2 * dim + 1:2 * dim + 2, lanes], (nz, LANES))
        return lanes, speed, gain, speed > 0

    def yz_tile(now, layer, index, _):
        x = layer(index // tiles)
        lanes, speed2, gain2, ahead2 = constants(index % tiles, 1)
        _, speed3, gain3, ahead3 = constants(index % tiles, 2)

        cells = [state[now, x, y, :, lanes] for y in range(ny)]
        f_low, f_mid, f, f_up = cells[-2], cells[-1], cells[0], cells[1]
        d = f - f_mid
        l_low = f_mid + gain2 * minmod(f_mid - f_low, d)
        d_up = f_up - f
        l = f + gain2 * minmod(d, d_up)
        change = l - l_low
        for y in range(ny):
            f, f_up, f_next = cells[y], cells[(y + 1) % ny], cells[(y + 2) % ny]
            d_next = f_next - f_up
            l_up = f_up + gain2 * minmod(d_up, d_next)
            change_up = l_up - l
            result = f - speed2 * jnp.where(ahead2, change, change_up)
            dz = pltpu.roll(f, nz - 1, 0) - f
            lz = f + gain3 * minmod(pltpu.roll(dz, 1, 0), dz)
            face = jnp.where(ahead3, lz, pltpu.roll(lz, nz - 1, 0))
            part[x, y, :, lanes] = result - speed3 * (face - pltpu.roll(face, 1, 0))
            d_up = d_next
            l, change = l_up, change_up
        return 0

    def yz(now, layer, count):
        lax.fori_loop(0, count * tiles, functools.partial(yz_tile, now, layer), 0)

    def x_tile(jobs, j, ys):
        lanes, speed, gain, ahead = constants(j, 0)
        for y in ys:
            for sources, outputs in jobs:
                f = [ref[(*lead, y, slice(None), lanes)] for ref, lead in sources]
                d = [b - a for a, b in zip(f[:-1], f[1:])]
                l = [f[i + 1] + gain * minmod(d[i], d[i + 1]) for i in range(len(d) - 1)]
                c = [b - a for a, b in zip(l[:-1], l[1:])]
                for i, x in enumerate(outputs):
                    moved[x, y, :, lanes] = part[x, y, :, lanes] - speed * jnp.where(
                        ahead, c[i], c[i + 1]
                    )

    yu = yc // 2

    def x_inner(now):
        job = ([(state, (now, x)) for x in range(rows)], range(2, rows - 2))

        def tile(index, _):
            x_tile([job], index % tiles, [(index // tiles) * yu + k for k in range(yu)])
            return 0

        lax.fori_loop(0, (ny // yu) * tiles, tile, 0)

    def x_outer(t, now, chunk):
        low = [(halo_low, (t, 0)), (halo_low, (t, 1))] + [(state, (now, x)) for x in range(4)]
        high = [(state, (now, x)) for x in range(rows - 4, rows)] + [
            (halo_high, (t, 0)), (halo_high, (t, 1))
        ]
        jobs = [(low, (0, 1)), (high, (rows - 2, rows - 1))]

        def tile(index, _):
            first = chunk * yc + (index // tiles) * yu
            x_tile(jobs, index % tiles, [first + k for k in range(yu)])
            return 0

        lax.fori_loop(0, (yc // yu) * tiles, tile, 0)

    def block_moments(places):
        flat = jnp.concatenate(
            [moved[x, pl.ds(c * yc, yc)].reshape(LANES, width) for x, c in places], axis=0
        )
        high = flat.astype(jnp.bfloat16)
        low = (flat - high.astype(jnp.float32)).astype(jnp.bfloat16)
        sums = jnp.dot(
            jnp.concatenate([high, low], axis=0), feat[...], preferred_element_type=jnp.float32
        )
        count = len(places) * LANES
        sums = sums[:count] + sums[count:]
        return [sums[k * LANES:(k + 1) * LANES].T[0:8] for k in range(len(places))]

    def outer_copy(t, c, p):
        return pltpu.make_async_remote_copy(
            src_ref=mom_outer.at[t, mv, c],
            dst_ref=mom_outer.at[t, mv, c],
            send_sem=outer_send.at[t, c, p - 1],
            recv_sem=outer_recv.at[t, c, p - 1],
            device_id={"vert": lax.rem(mv + p, nv)},
            device_id_type=MESH,
        )

    def inner_copy(t, p):
        return pltpu.make_async_remote_copy(
            src_ref=mom_inner.at[t, mv],
            dst_ref=mom_inner.at[t, mv],
            send_sem=inner_send.at[t, p - 1],
            recv_sem=inner_recv.at[t, p - 1],
            device_id={"vert": lax.rem(mv + p, nv)},
            device_id_type=MESH,
        )

    def moments_outer(t, c):
        for i, x in enumerate(outer_layers):
            mom_outer[t, mv, c, i] = block_moments([(x, c)])[0]
        for p in range(1, nv):
            outer_copy(t, c, p).start()

    def moments_inner(t):
        def layer(i, _):
            for c, sums in enumerate(block_moments([(i + 2, c) for c in range(chunks)])):
                mom_inner[t, mv, i * chunks + c] = sums
            return 0

        lax.fori_loop(0, inner_rows, layer, 0)
        for p in range(1, nv):
            inner_copy(t, p).start()

    def coefficients(blocks, first):
        sums = jnp.concatenate(
            [functools.reduce(lambda a, b: a + b, parts) for parts in blocks], axis=1
        )
        count = len(blocks)
        code = jnp.concatenate([cell_code[first + k] for k in range(count)], axis=1)
        weight = sums[0:1]
        density = weight / total
        inverse = 1.0 / weight
        u1 = H1 * sums[1:2] * inverse
        u2 = H2 * sums[2:3] * inverse
        u3 = H3 * sums[3:4] * inverse
        square = (H1 * H1) * (sums[4:5] + sums[5:6] + sums[6:7]) * inverse
        temperature = (square - (u1 * u1 + u2 * u2 + u3 * u3)) / 3.0
        is_inflow = code == 1.0
        is_wall = code == 2.0
        is_open = code == 0.0
        rate = 0.5 * density / (density + knudsen[0:1, 0:1])
        zero = jnp.zeros_like(u1)
        u1 = jnp.where(is_inflow, inflow[0:1, 1:2], jnp.where(is_wall, zero, u1))
        u2 = jnp.where(is_open, u2, zero)
        u3 = jnp.where(is_open, u3, zero)
        temperature = jnp.where(
            is_inflow, inflow[0:1, 2:3], jnp.where(is_wall, inflow[0:1, 3:4], temperature)
        )
        front = jnp.where(
            is_inflow, inflow[0:1, 0:1], jnp.where(is_wall, density, rate * density)
        )
        keep = jnp.where(is_open, 1.0 - rate, zero)
        sharp = (0.5 * LOG2E) / temperature

        def axis_sum(points, spacing, u):
            grid = lax.broadcasted_iota(jnp.int32, (points, count * LANES), 0)
            away = (2.0 * grid.astype(jnp.float32) + (1.0 - points)) * spacing - u
            return jnp.sum(jnp.exp2(-(away * away) * sharp), axis=0, keepdims=True)

        norm = axis_sum(VGX, H1, u1) * axis_sum(VGY, H2, u2) * axis_sum(VGZ, H3, u3)
        constant = jnp.log2(front * total / norm) - (u1 * u1 + u2 * u2 + u3 * u3) * sharp
        slope = 2.0 * sharp
        quad = -(H1 * H1) * sharp
        packed = jnp.concatenate(
            [
                constant, slope * u1 * H1, slope * u2 * H2, slope * u3 * H3,
                quad, quad, quad, keep,
            ],
            axis=0,
        )
        stacked = jnp.concatenate([*split3(packed), jnp.zeros_like(packed)], axis=0)
        for k in range(count):
            coef[first + k] = stacked[:, k * LANES:(k + 1) * LANES].T.astype(jnp.bfloat16)

    def relax_block(then, k, x, c):
        ys = pl.ds(c * yc, yc)
        power = jnp.dot(coef[k], wide[...], preferred_element_type=jnp.float32)
        keep = power[:, width:]
        for j in range(tiles):
            lanes = slice(j * LANES, (j + 1) * LANES)
            old = moved[x, ys, :, lanes]
            new = keep * old.reshape(LANES, LANES) + jnp.exp2(power[:, lanes])
            state[then, x, ys, :, lanes] = new.reshape(old.shape)

    def relax_outer(t, then, c):
        for p in range(1, nv):
            outer_copy(t, c, p).wait_recv()
        coefficients(
            [[mom_outer[t, v, c, i] for v in range(nv)] for i in range(4)], 4 * c
        )
        for i, x in enumerate(outer_layers):
            relax_block(then, 4 * c + i, x, c)

    def relax_inner(t, then):
        for p in range(1, nv):
            inner_copy(t, p).wait_recv()
        coefficients(
            [[mom_inner[t, v, k] for v in range(nv)] for k in range(inner_blocks)], 4 * chunks
        )

        def layer(i, _):
            for c in range(chunks):
                relax_block(then, 4 * chunks + i * chunks + c, i + 2, c)
            return 0

        lax.fori_loop(0, inner_rows, layer, 0)

    final = STEPS % 2

    def write_inner():
        xs = pl.ds(2, inner_rows)
        return pltpu.make_async_copy(state.at[final, xs], out.at[xs], out_sem.at[0])

    def write_outer(c, side):
        xs, ys = pl.ds(side * (rows - 2), 2), pl.ds(c * yc, yc)
        return pltpu.make_async_copy(
            state.at[final, xs, ys], out.at[xs, ys], out_sem.at[1 + 2 * c + side]
        )

    def outer_layer(i):
        return i + inner_rows * (i // 2)

    def step(t, _):
        last = t == STEPS - 1
        now = t % 2
        then = 1 - now
        current = state.at[now]
        following = state.at[then]
        split = inner_rows // 2

        def fill_early():
            yz(now, lambda i: i + 2, split)

        def fill_between():
            yz(now, lambda i: i + 2 + split, inner_rows - split)
            x_inner(now)
            moments_inner(t)
            fill_late()

        def fill_late():
            relax_inner(t, then)

        yz(now, outer_layer, 4)
        for c in range(chunks):

            @pl.when(has_high)
            def _():
                to_low(t, c, current).wait_recv()

            @pl.when(has_low)
            def _():
                to_high(t, c, current).wait_recv()

            x_outer(t, now, c)
            moments_outer(t, c)
            if c == 0:
                fill_early()
            @pl.when(last)
            def _():
                if c == chunks - 1:
                    write_inner().start()

            relax_outer(t, then, c)

            @pl.when(jnp.logical_and(has_low, jnp.logical_not(last)))
            def _():
                to_low(t + 1, c, following).start()

            @pl.when(jnp.logical_and(has_high, jnp.logical_not(last)))
            def _():
                to_high(t + 1, c, following).start()

            @pl.when(last)
            def _():
                for side in range(2):
                    write_outer(c, side).start()

            if c == 0:
                fill_between()

        for c in range(chunks):

            @pl.when(has_low)
            def _():
                to_low(t, c, current).wait_send()

            @pl.when(has_high)
            def _():
                to_high(t, c, current).wait_send()

            for p in range(1, nv):
                outer_copy(t, c, p).wait_send()
        for p in range(1, nv):
            inner_copy(t, p).wait_send()
        return 0

    lax.fori_loop(0, STEPS, step, 0)
    write_inner().wait()
    for c in range(chunks):
        for side in range(2):
            write_outer(c, side).wait()


def body(distribution, velocity_order, cell_codes, knudsen, inflow):
    rows, ny, nz, width = distribution.shape
    nv = lax.axis_size("vert")
    nx_dev = lax.axis_size("gx")
    chunks = ny * nz // LANES
    inner_blocks = (rows - 4) * chunks
    blocks = 4 * chunks + inner_blocks
    hbm = pl.BlockSpec(memory_space=pl.ANY)
    dma = pltpu.SemaphoreType.DMA
    return pl.pallas_call(
        functools.partial(kernel, rows, ny, nz, width, nx_dev, nv),
        out_shape=jax.ShapeDtypeStruct(distribution.shape, jnp.float32),
        in_specs=[pl.BlockSpec(memory_space=pltpu.HBM)] * 5,
        out_specs=hbm,
        scratch_shapes=[
            pltpu.VMEM((2, rows, ny, nz, width), jnp.float32),
            pltpu.VMEM((rows, ny, nz, width), jnp.float32),
            pltpu.VMEM((rows, ny, nz, width), jnp.float32),
            pltpu.VMEM((STEPS, 2, ny, nz, width), jnp.float32),
            pltpu.VMEM((STEPS, 2, ny, nz, width), jnp.float32),
            pltpu.VMEM((STEPS, nv, chunks, 4, 8, LANES), jnp.float32),
            pltpu.VMEM((STEPS, nv, inner_blocks, 8, LANES), jnp.float32),
            pltpu.VMEM((blocks, LANES, 32), jnp.bfloat16),
            pltpu.VMEM((width, LANES), jnp.bfloat16),
            pltpu.VMEM((32, width + LANES), jnp.bfloat16),
            pltpu.VMEM((8, width), jnp.float32),
            pltpu.VMEM((1, width), jnp.int32),
            pltpu.VMEM((rows, ny, nz), jnp.int32),
            pltpu.VMEM((1, 1), jnp.float32),
            pltpu.VMEM((1, 4), jnp.float32),
            pltpu.VMEM((rows * ny, LANES), jnp.float32),
            pltpu.VMEM((blocks, 1, LANES), jnp.float32),
            dma((3,)),
            dma((4,)),
            dma((1 + 2 * chunks,)),
            dma((STEPS, 2, chunks)),
            dma((STEPS, 2, chunks)),
            dma((STEPS, chunks, nv - 1)),
            dma((STEPS, chunks, nv - 1)),
            dma((STEPS, nv - 1)),
            dma((STEPS, nv - 1)),
        ],
        compiler_params=pltpu.CompilerParams(
            collective_id=0, has_side_effects=True, vmem_limit_bytes=48 * 1024 * 1024
        ),
    )(
        distribution,
        velocity_order.reshape(1, width),
        cell_codes,
        knudsen.reshape(1, 1),
        inflow.reshape(1, 4),
    )


def solution(mesh):
    placed = (
        P(("groups", "gx"), None, None, "vert"),
        P("vert"),
        P(("groups", "gx"), None, None),
        P("groups"),
        P("groups"),
    )
    return jax.shard_map(
        body,
        mesh=mesh,
        in_specs=placed,
        out_specs=P(("groups", "gx"), None, None, "vert"),
        check_vma=False,
    )
```

```python
import functools

import jax
import jax.numpy as jnp
from jax import lax
from jax.experimental import pallas as pl
from jax.experimental.pallas import tpu as pltpu
from jax.sharding import PartitionSpec as P

VGX = 16
VGY = 16
VGZ = 8
STEPS = 3
LANES = 128
LOG2E = 1.4426950408889634
MESH = pl.DeviceIdType.MESH

H1 = 3.0 / VGX
H2 = 3.0 / VGY
H3 = 3.0 / VGZ


def minmod(lower, upper):
    return jnp.maximum(jnp.minimum(lower, upper), jnp.minimum(jnp.maximum(lower, upper), 0.0))


def split3(value):
    high = value.astype(jnp.bfloat16).astype(jnp.float32)
    rest = value - high
    middle = rest.astype(jnp.bfloat16).astype(jnp.float32)
    return high, middle, rest - middle


def kernel(
    rows, ny, nz, width, nx_dev, nv,
    dist, order_in, codes_in, knudsen_in, inflow_in,
    out,
    state, part, moved, halo_low, halo_high, mom_outer, mom_inner, coef, feat, wide, cour,
    order, codes, knudsen, inflow, spread, cell_code,
    in_sem, small_sem, out_sem, halo_send, halo_recv,
    outer_send, outer_recv, inner_send, inner_recv,
):
    tiles = width // LANES
    total = float(width * nv)
    yc = LANES // nz
    chunks = ny // yc
    inner_rows = rows - 4
    inner_blocks = inner_rows * chunks
    outer_layers = (0, 1, rows - 2, rows - 1)
    mx = lax.axis_index("gx")
    mv = lax.axis_index("vert")
    has_low = mx > 0
    has_high = mx < nx_dev - 1

    small = [
        pltpu.make_async_copy(source, target, small_sem.at[i])
        for i, (source, target) in enumerate(
            ((order_in, order), (codes_in, codes), (knudsen_in, knudsen), (inflow_in, inflow))
        )
    ]
    for copy in small:
        copy.start()
    load = [
        pltpu.make_async_copy(
            dist.at[pl.ds(first, count)], state.at[0, pl.ds(first, count)], in_sem.at[i]
        )
        for i, (first, count) in enumerate(((0, 2), (rows - 2, 2), (2, inner_rows)))
    ]
    for copy in load:
        copy.start()

    barrier = pltpu.get_barrier_semaphore()

    @pl.when(has_low)
    def _():
        pl.semaphore_signal(barrier, inc=1, device_id={"gx": mx - 1}, device_id_type=MESH)

    @pl.when(has_high)
    def _():
        pl.semaphore_signal(barrier, inc=1, device_id={"gx": mx + 1}, device_id_type=MESH)

    for p in range(1, nv):
        pl.semaphore_signal(
            barrier, inc=1, device_id={"vert": lax.rem(mv + p, nv)}, device_id_type=MESH
        )
    pl.semaphore_wait(
        barrier, nv - 1 + has_low.astype(jnp.int32) + has_high.astype(jnp.int32)
    )

    def to_low(t, c, source):
        ys = pl.ds(c * yc, yc)
        return pltpu.make_async_remote_copy(
            src_ref=source.at[pl.ds(0, 2), ys],
            dst_ref=halo_high.at[t, :, ys],
            send_sem=halo_send.at[t, 0, c],
            recv_sem=halo_recv.at[t, 0, c],
            device_id={"gx": mx - 1},
            device_id_type=MESH,
        )

    def to_high(t, c, source):
        ys = pl.ds(c * yc, yc)
        return pltpu.make_async_remote_copy(
            src_ref=source.at[pl.ds(rows - 2, 2), ys],
            dst_ref=halo_low.at[t, :, ys],
            send_sem=halo_send.at[t, 1, c],
            recv_sem=halo_recv.at[t, 1, c],
            device_id={"gx": mx + 1},
            device_id_type=MESH,
        )

    @pl.when(has_low)
    def _():
        for c in range(chunks):
            to_low(0, c, dist).start()

    @pl.when(has_high)
    def _():
        for c in range(chunks):
            to_high(0, c, dist).start()

    for copy in small:
        copy.wait()

    slot = order[...]
    odd1 = (2 * (slot // (VGY * VGZ)) + 1 - VGX).astype(jnp.float32)
    odd2 = (2 * ((slot // VGZ) % VGY) + 1 - VGY).astype(jnp.float32)
    odd3 = (2 * (slot % VGZ) + 1 - VGZ).astype(jnp.float32)
    ratio = (H3 / H1) ** 2
    table = jnp.concatenate(
        [
            jnp.ones_like(odd1), odd1, odd2, odd3,
            odd1 * odd1, odd2 * odd2, ratio * odd3 * odd3, jnp.zeros_like(odd1),
        ],
        axis=0,
    )
    rest = jnp.zeros((LANES - 8, width), jnp.float32)
    feat[...] = jnp.concatenate([table, rest], axis=0).T.astype(jnp.bfloat16)
    keep_row = (lax.broadcasted_iota(jnp.int32, (8, LANES), 0) == 7).astype(jnp.float32)
    broad = jnp.concatenate([table, keep_row], axis=1)
    wide[...] = jnp.concatenate([broad, broad, broad, jnp.zeros_like(broad)], axis=0).astype(
        jnp.bfloat16
    )
    speeds = []
    for speed in (0.1 * H1 * odd1, (H2 / 30.0) * odd2, (H3 / 30.0) * odd3):
        gain = 0.5 * (1.0 - jnp.abs(speed)) * jnp.where(speed > 0, 1.0, -1.0)
        speeds += [speed, gain]
    cour[...] = jnp.concatenate(speeds + [jnp.zeros_like(odd1)] * 2, axis=0)

    pick = lax.broadcasted_iota(jnp.int32, (nz, LANES), 1) % nz
    pick = (pick == lax.broadcasted_iota(jnp.int32, (nz, LANES), 0)).astype(jnp.bfloat16)
    spread[...] = jnp.dot(
        codes[...].reshape(rows * ny, nz).astype(jnp.float32).astype(jnp.bfloat16),
        pick,
        preferred_element_type=jnp.float32,
    )

    own_line = lax.broadcasted_iota(jnp.int32, (yc, LANES), 0)
    own_line = own_line == lax.broadcasted_iota(jnp.int32, (yc, LANES), 1) // nz
    places = [(x, c) for c in range(chunks) for x in outer_layers]
    places += [(x, c) for x in range(2, rows - 2) for c in range(chunks)]
    for k, (x, c) in enumerate(places):
        row = x * ny + c * yc
        cell_code[k] = jnp.sum(
            jnp.where(own_line, spread[row:row + yc], 0.0), axis=0, keepdims=True
        )

    @pl.when(jnp.logical_not(has_low))
    def _():
        halo_low[...] = jnp.zeros_like(halo_low)

    @pl.when(jnp.logical_not(has_high))
    def _():
        halo_high[...] = jnp.zeros_like(halo_high)

    for copy in load:
        copy.wait()

    def constants(j, dim):
        lanes = pl.ds(pl.multiple_of(j * LANES, LANES), LANES)
        speed = jnp.broadcast_to(cour[2 * dim:2 * dim + 1, lanes], (nz, LANES))
        gain = jnp.broadcast_to(cour[2 * dim + 1:2 * dim + 2, lanes], (nz, LANES))
        return lanes, speed, gain, speed > 0

    def yz_tile(now, layer, index, _):
        x = layer(index // tiles)
        lanes, speed2, gain2, ahead2 = constants(index % tiles, 1)
        _, speed3, gain3, ahead3 = constants(index % tiles, 2)

        cells = [state[now, x, y, :, lanes] for y in range(ny)]
        f_low, f_mid, f, f_up = cells[-2], cells[-1], cells[0], cells[1]
        d = f - f_mid
        l_low = f_mid + gain2 * minmod(f_mid - f_low, d)
        d_up = f_up - f
        l = f + gain2 * minmod(d, d_up)
        change = l - l_low
        for y in range(ny):
            f, f_up, f_next = cells[y], cells[(y + 1) % ny], cells[(y + 2) % ny]
            d_next = f_next - f_up
            l_up = f_up + gain2 * minmod(d_up, d_next)
            change_up = l_up - l
            result = f - speed2 * jnp.where(ahead2, change, change_up)
            dz = pltpu.roll(f, nz - 1, 0) - f
            lz = f + gain3 * minmod(pltpu.roll(dz, 1, 0), dz)
            face = jnp.where(ahead3, lz, pltpu.roll(lz, nz - 1, 0))
            part[x, y, :, lanes] = result - speed3 * (face - pltpu.roll(face, 1, 0))
            d_up = d_next
            l, change = l_up, change_up
        return 0

    def yz(now, layer, count):
        lax.fori_loop(0, count * tiles, functools.partial(yz_tile, now, layer), 0)

    def x_tile(jobs, j, ys):
        lanes, speed, gain, ahead = constants(j, 0)
        for y in ys:
            for sources, outputs in jobs:
                f = [ref[(*lead, y, slice(None), lanes)] for ref, lead in sources]
                d = [b - a for a, b in zip(f[:-1], f[1:])]
                l = [f[i + 1] + gain * minmod(d[i], d[i + 1]) for i in range(len(d) - 1)]
                c = [b - a for a, b in zip(l[:-1], l[1:])]
                for i, x in enumerate(outputs):
                    moved[x, y, :, lanes] = part[x, y, :, lanes] - speed * jnp.where(
                        ahead, c[i], c[i + 1]
                    )

    yu = yc // 2

    def x_inner(now):
        job = ([(state, (now, x)) for x in range(rows)], range(2, rows - 2))

        def tile(index, _):
            x_tile([job], index % tiles, [(index // tiles) * yu + k for k in range(yu)])
            return 0

        lax.fori_loop(0, (ny // yu) * tiles, tile, 0)

    def x_outer(t, now, chunk):
        low = [(halo_low, (t, 0)), (halo_low, (t, 1))] + [(state, (now, x)) for x in range(4)]
        high = [(state, (now, x)) for x in range(rows - 4, rows)] + [
            (halo_high, (t, 0)), (halo_high, (t, 1))
        ]
        jobs = [(low, (0, 1)), (high, (rows - 2, rows - 1))]

        def tile(index, _):
            first = chunk * yc + (index // tiles) * yu
            x_tile(jobs, index % tiles, [first + k for k in range(yu)])
            return 0

        lax.fori_loop(0, (yc // yu) * tiles, tile, 0)

    def block_moments(x, c):
        flat = moved[x, pl.ds(c * yc, yc)].reshape(LANES, width)
        high = flat.astype(jnp.bfloat16)
        low = (flat - high.astype(jnp.float32)).astype(jnp.bfloat16)
        sums = jnp.dot(high, feat[...], preferred_element_type=jnp.float32) + jnp.dot(
            low, feat[...], preferred_element_type=jnp.float32
        )
        return sums.T[0:8]

    def outer_copy(t, c, p):
        return pltpu.make_async_remote_copy(
            src_ref=mom_outer.at[t, mv, c],
            dst_ref=mom_outer.at[t, mv, c],
            send_sem=outer_send.at[t, c, p - 1],
            recv_sem=outer_recv.at[t, c, p - 1],
            device_id={"vert": lax.rem(mv + p, nv)},
            device_id_type=MESH,
        )

    def inner_copy(t, p):
        return pltpu.make_async_remote_copy(
            src_ref=mom_inner.at[t, mv],
            dst_ref=mom_inner.at[t, mv],
            send_sem=inner_send.at[t, p - 1],
            recv_sem=inner_recv.at[t, p - 1],
            device_id={"vert": lax.rem(mv + p, nv)},
            device_id_type=MESH,
        )

    def moments_outer(t, c):
        for i, x in enumerate(outer_layers):
            mom_outer[t, mv, c, i] = block_moments(x, c)
        for p in range(1, nv):
            outer_copy(t, c, p).start()

    def moments_inner(t):
        def layer(i, _):
            for c in range(chunks):
                mom_inner[t, mv, i * chunks + c] = block_moments(i + 2, c)
            return 0

        lax.fori_loop(0, inner_rows, layer, 0)
        for p in range(1, nv):
            inner_copy(t, p).start()

    def coefficients(blocks, first):
        sums = jnp.concatenate(
            [functools.reduce(lambda a, b: a + b, parts) for parts in blocks], axis=1
        )
        count = len(blocks)
        code = jnp.concatenate([cell_code[first + k] for k in range(count)], axis=1)
        weight = sums[0:1]
        density = weight / total
        inverse = 1.0 / weight
        u1 = H1 * sums[1:2] * inverse
        u2 = H2 * sums[2:3] * inverse
        u3 = H3 * sums[3:4] * inverse
        square = (H1 * H1) * (sums[4:5] + sums[5:6] + sums[6:7]) * inverse
        temperature = (square - (u1 * u1 + u2 * u2 + u3 * u3)) / 3.0
        is_inflow = code == 1.0
        is_wall = code == 2.0
        is_open = code == 0.0
        rate = 0.5 * density / (density + knudsen[0:1, 0:1])
        zero = jnp.zeros_like(u1)
        u1 = jnp.where(is_inflow, inflow[0:1, 1:2], jnp.where(is_wall, zero, u1))
        u2 = jnp.where(is_open, u2, zero)
        u3 = jnp.where(is_open, u3, zero)
        temperature = jnp.where(
            is_inflow, inflow[0:1, 2:3], jnp.where(is_wall, inflow[0:1, 3:4], temperature)
        )
        front = jnp.where(
            is_inflow, inflow[0:1, 0:1], jnp.where(is_wall, density, rate * density)
        )
        keep = jnp.where(is_open, 1.0 - rate, zero)
        sharp = (0.5 * LOG2E) / temperature

        def axis_sum(points, spacing, u):
            grid = lax.broadcasted_iota(jnp.int32, (points, count * LANES), 0)
            away = (2.0 * grid.astype(jnp.float32) + (1.0 - points)) * spacing - u
            return jnp.sum(jnp.exp2(-(away * away) * sharp), axis=0, keepdims=True)

        norm = axis_sum(VGX, H1, u1) * axis_sum(VGY, H2, u2) * axis_sum(VGZ, H3, u3)
        constant = jnp.log2(front * total / norm) - (u1 * u1 + u2 * u2 + u3 * u3) * sharp
        slope = 2.0 * sharp
        quad = -(H1 * H1) * sharp
        packed = jnp.concatenate(
            [
                constant, slope * u1 * H1, slope * u2 * H2, slope * u3 * H3,
                quad, quad, quad, keep,
            ],
            axis=0,
        )
        stacked = jnp.concatenate([*split3(packed), jnp.zeros_like(packed)], axis=0)
        for k in range(count):
            coef[first + k] = stacked[:, k * LANES:(k + 1) * LANES].T.astype(jnp.bfloat16)

    def relax_block(then, k, x, c):
        ys = pl.ds(c * yc, yc)
        power = jnp.dot(coef[k], wide[...], preferred_element_type=jnp.float32)
        keep = power[:, width:]
        for j in range(tiles):
            lanes = slice(j * LANES, (j + 1) * LANES)
            old = moved[x, ys, :, lanes]
            new = keep * old.reshape(LANES, LANES) + jnp.exp2(power[:, lanes])
            state[then, x, ys, :, lanes] = new.reshape(old.shape)

    def relax_outer(t, then, c):
        for p in range(1, nv):
            outer_copy(t, c, p).wait_recv()
        coefficients(
            [[mom_outer[t, v, c, i] for v in range(nv)] for i in range(4)], 4 * c
        )
        for i, x in enumerate(outer_layers):
            relax_block(then, 4 * c + i, x, c)

    def relax_inner(t, then):
        for p in range(1, nv):
            inner_copy(t, p).wait_recv()
        coefficients(
            [[mom_inner[t, v, k] for v in range(nv)] for k in range(inner_blocks)], 4 * chunks
        )

        def layer(i, _):
            for c in range(chunks):
                relax_block(then, 4 * chunks + i * chunks + c, i + 2, c)
            return 0

        lax.fori_loop(0, inner_rows, layer, 0)

    final = STEPS % 2

    def write_inner():
        xs = pl.ds(2, inner_rows)
        return pltpu.make_async_copy(state.at[final, xs], out.at[xs], out_sem.at[0])

    def write_outer(c, side):
        xs, ys = pl.ds(side * (rows - 2), 2), pl.ds(c * yc, yc)
        return pltpu.make_async_copy(
            state.at[final, xs, ys], out.at[xs, ys], out_sem.at[1 + 2 * c + side]
        )

    def outer_layer(i):
        return i + inner_rows * (i // 2)

    def step(t, _):
        last = t == STEPS - 1
        now = t % 2
        then = 1 - now
        current = state.at[now]
        following = state.at[then]
        def arrive(c):
            @pl.when(has_high)
            def _():
                to_low(t, c, current).wait_recv()

            @pl.when(has_low)
            def _():
                to_high(t, c, current).wait_recv()

            x_outer(t, now, c)
            moments_outer(t, c)

        def leave(c):
            relax_outer(t, then, c)

            @pl.when(jnp.logical_and(has_low, jnp.logical_not(last)))
            def _():
                to_low(t + 1, c, following).start()

            @pl.when(jnp.logical_and(has_high, jnp.logical_not(last)))
            def _():
                to_high(t + 1, c, following).start()

            @pl.when(last)
            def _():
                for side in range(2):
                    write_outer(c, side).start()

        yz(now, outer_layer, 4)
        for c in range(chunks - 1):
            arrive(c)
        yz(now, lambda i: i + 2, inner_rows)
        x_inner(now)
        moments_inner(t)
        arrive(chunks - 1)
        for c in range(chunks - 1):
            leave(c)
        relax_inner(t, then)

        @pl.when(last)
        def _():
            write_inner().start()

        leave(chunks - 1)

        for c in range(chunks):

            @pl.when(has_low)
            def _():
                to_low(t, c, current).wait_send()

            @pl.when(has_high)
            def _():
                to_high(t, c, current).wait_send()

            for p in range(1, nv):
                outer_copy(t, c, p).wait_send()
        for p in range(1, nv):
            inner_copy(t, p).wait_send()
        return 0

    lax.fori_loop(0, STEPS, step, 0)
    write_inner().wait()
    for c in range(chunks):
        for side in range(2):
            write_outer(c, side).wait()


def body(distribution, velocity_order, cell_codes, knudsen, inflow):
    rows, ny, nz, width = distribution.shape
    nv = lax.axis_size("vert")
    nx_dev = lax.axis_size("gx")
    chunks = ny * nz // LANES
    inner_blocks = (rows - 4) * chunks
    blocks = 4 * chunks + inner_blocks
    hbm = pl.BlockSpec(memory_space=pl.ANY)
    dma = pltpu.SemaphoreType.DMA
    return pl.pallas_call(
        functools.partial(kernel, rows, ny, nz, width, nx_dev, nv),
        out_shape=jax.ShapeDtypeStruct(distribution.shape, jnp.float32),
        in_specs=[pl.BlockSpec(memory_space=pltpu.HBM)] * 5,
        out_specs=hbm,
        scratch_shapes=[
            pltpu.VMEM((2, rows, ny, nz, width), jnp.float32),
            pltpu.VMEM((rows, ny, nz, width), jnp.float32),
            pltpu.VMEM((rows, ny, nz, width), jnp.float32),
            pltpu.VMEM((STEPS, 2, ny, nz, width), jnp.float32),
            pltpu.VMEM((STEPS, 2, ny, nz, width), jnp.float32),
            pltpu.VMEM((STEPS, nv, chunks, 4, 8, LANES), jnp.float32),
            pltpu.VMEM((STEPS, nv, inner_blocks, 8, LANES), jnp.float32),
            pltpu.VMEM((blocks, LANES, 32), jnp.bfloat16),
            pltpu.VMEM((width, LANES), jnp.bfloat16),
            pltpu.VMEM((32, width + LANES), jnp.bfloat16),
            pltpu.VMEM((8, width), jnp.float32),
            pltpu.VMEM((1, width), jnp.int32),
            pltpu.VMEM((rows, ny, nz), jnp.int32),
            pltpu.VMEM((1, 1), jnp.float32),
            pltpu.VMEM((1, 4), jnp.float32),
            pltpu.VMEM((rows * ny, LANES), jnp.float32),
            pltpu.VMEM((blocks, 1, LANES), jnp.float32),
            dma((3,)),
            dma((4,)),
            dma((1 + 2 * chunks,)),
            dma((STEPS, 2, chunks)),
            dma((STEPS, 2, chunks)),
            dma((STEPS, chunks, nv - 1)),
            dma((STEPS, chunks, nv - 1)),
            dma((STEPS, nv - 1)),
            dma((STEPS, nv - 1)),
        ],
        compiler_params=pltpu.CompilerParams(
            collective_id=0, has_side_effects=True, vmem_limit_bytes=48 * 1024 * 1024
        ),
    )(
        distribution,
        velocity_order.reshape(1, width),
        cell_codes,
        knudsen.reshape(1, 1),
        inflow.reshape(1, 4),
    )


def solution(mesh):
    placed = (
        P(("groups", "gx"), None, None, "vert"),
        P("vert"),
        P(("groups", "gx"), None, None),
        P("groups"),
        P("groups"),
    )
    return jax.shard_map(
        body,
        mesh=mesh,
        in_specs=placed,
        out_specs=P(("groups", "gx"), None, None, "vert"),
        check_vma=False,
    )
```
